32 devices in a mesh: rows: 8 (over z, x), cols: 4 (over y, core).
Axes of the slice: x: 2, y: 2, z: 4, core: 2. Of those that a mesh axis runs over, the one named last changes fastest.
Arguments:
- matrix: float32 [16384, 1024], P('rows', 'cols'), may hold values from -80 to 80
- gaussian: float32 [256, 16384], P(None, 'rows'), may hold values from -0.0625 to 0.0625
- pivots: int32 [256], replicated, may hold values from 0 to 1023, as said below
- trailing: float32 [16384, 512], P('rows', 'cols'), may hold values from -6 to 6
Outputs:
- sketch: float32 [256, 1024], P('rows', 'cols')
- coupling: float32 [256, 512], P(None, 'cols')
- projected: float32 [16384, 512], P('rows', 'cols')
- trailing_sketch: float32 [256, 512], P('rows', 'cols')
The draws below stay inside these ranges and needn't reach their ends.
Inputs may be any that keep to these rules, and one draw needn't show every extreme that they name: `pivots`: 256 distinct column indices; at most 64 of them lie in one block of 256 consecutive columns starting at a multiple of 256, and exactly 64 in some such block.
All inputs are finite; a program needn't handle non-finite values.
Results may differ from the reference program's by a relative error of at most 0.00015.
Values sent between devices are 32-bit elements; how exact they have to be, the bound alone decides.
A program may use at most 64 MiB of HBM per device.

```python
import math
import jax
import jax.numpy as jnp
from jax import lax

COLS_DEV = 256
SKETCH = 256
PANEL = 256
SLAB = 512
MOST = 64
M = 16384
N = 1024


def draw_matrix(key, part):
    key = jax.random.fold_in(key, 11)
    keys = jax.random.split(key, 3)
    position = jnp.arange(M, dtype=jnp.float32) / M
    row_scale = jnp.exp(jax.random.uniform(keys[0], (M, 1), jnp.float32, math.log(0.3), math.log(3.0)))
    row_scale = row_scale * jnp.exp(math.log(3.0) * (position - 0.5))[:, None]
    col_scale = jnp.exp(jax.random.uniform(keys[1], (1, N), jnp.float32, math.log(0.3), math.log(3.0)))
    base_values = jnp.clip(jax.random.normal(keys[2], (M, N), jnp.float32), -5.0, 5.0)
    return base_values * row_scale * col_scale


def draw_pivots(key, part):
    key = jax.random.fold_in(key, 5)
    keys = jax.random.split(key, 4)
    blocks = N // COLS_DEV
    busiest = jax.random.randint(keys[0], (), 0, blocks)
    scores = jax.random.randint(keys[1], (blocks, COLS_DEV), 0, 1 << 20) * COLS_DEV + jnp.arange(COLS_DEV)[None, :]
    ranking = jnp.argsort(scores, axis=1).astype(jnp.int32)
    busy_cols = busiest * COLS_DEV + jnp.take(ranking, busiest, axis=0)[:MOST]
    chosen = jax.random.permutation(keys[2], (blocks - 1) * MOST)[:PANEL - MOST]
    owner_block = chosen // MOST
    owner_block = owner_block + (owner_block >= busiest).astype(jnp.int32)
    other_cols = owner_block * COLS_DEV + ranking[owner_block, chosen % MOST]
    together = jnp.concatenate([busy_cols, other_cols]).astype(jnp.int32)
    return jax.random.permutation(keys[3], together).astype(jnp.int32)


def with_spikes(drawn, rng, source, target, shards_of, factor):
    owner, partner = [(jnp.arange(drawn.shape[axis_at]) // (drawn.shape[axis_at] // shards_of)).reshape([-1 if axis == axis_at else 1 for axis in range(drawn.ndim)]) for axis_at in (source, target)]
    chosen = jax.random.permutation(rng, shards_of)[partner]
    strong = (owner == chosen) | (owner == (partner + shards_of // 2) % shards_of)
    return jnp.where(strong, factor * drawn, drawn)


def block_scale(rng, extent, pieces, low, top_value):
    factor_of = 1.0
    for dim, blocks in pieces:
        steps = jax.random.uniform(jax.random.fold_in(jax.random.fold_in(rng, 6), dim), (blocks,), jnp.float32, low / len(pieces), top_value / len(pieces))
        factor_of = factor_of * jnp.repeat(jnp.exp(steps), extent[dim] // blocks).reshape((-1,) + (1,) * (len(extent) - 1 - dim))
    return factor_of


def noise(key, dims, scale, reach, cuts=(), kind=jnp.bfloat16):
    loudness = block_scale(key, dims, cuts, -0.22, 0.18) if cuts else 1.0
    result = jax.random.normal(key, dims, jnp.float32) * scale * loudness
    return jnp.minimum(jnp.maximum(result, -reach), reach).astype(kind)


def bell_draw_with(rng, extent, spread, reach, cuts, heavy, kind=jnp.bfloat16):
    array = spread * jax.random.normal(rng, extent, jnp.float32)
    if cuts:
        array = array * block_scale(rng, extent, cuts, -0.22, 0.18)
    return jnp.clip(with_spikes(array, jax.random.fold_in(rng, 3), *heavy), -reach, reach).astype(kind)


def setup_inputs(seed: int = 0) -> dict:
    streams_of = jax.random.split(jax.random.key(seed), 5)
    matrix = draw_matrix(jax.random.fold_in(streams_of[4], 71), 0)
    gaussian = bell_draw_with(streams_of[1], (SKETCH, M), M ** -0.5, 0.0625, ((1, 8),), (1, 0, 8, 2.0), jnp.float32)
    pivots = draw_pivots(jax.random.fold_in(streams_of[4], 71), 0)
    trailing = noise(streams_of[3], (M, SLAB), 1.0, 6.0, ((0, 8), (1, 4)), jnp.float32)
    return dict(matrix=matrix, gaussian=gaussian, pivots=pivots, trailing=trailing)


def inner_rows(left, right):
    return lax.dot_general(left.astype(jnp.float32), right.astype(jnp.float32), (((0,), (0,)), ((), ())), precision=lax.Precision.HIGHEST, preferred_element_type=jnp.float32)

def factor_parts(gram_matrix, cross_terms):
    chol_factor = jnp.linalg.cholesky(gram_matrix)
    coupling = lax.linalg.triangular_solve(chol_factor, cross_terms, left_side=True, lower=True)
    weights = lax.linalg.triangular_solve(chol_factor, coupling, left_side=True, lower=True, transpose_a=True)
    return (coupling, weights)

def reference(matrix, gaussian, pivots, trailing):
    highest = lax.Precision.HIGHEST
    sketch = jnp.dot(gaussian.astype(jnp.float32), matrix.astype(jnp.float32), precision=highest, preferred_element_type=jnp.float32)
    panel_block = jnp.take(matrix, pivots, axis=1)
    gram_matrix = inner_rows(panel_block, panel_block)
    cross_terms = inner_rows(panel_block, trailing)
    gauss_panel = jnp.dot(gaussian.astype(jnp.float32), panel_block.astype(jnp.float32), precision=highest, preferred_element_type=jnp.float32)
    gauss_trail = jnp.dot(gaussian.astype(jnp.float32), trailing.astype(jnp.float32), precision=highest, preferred_element_type=jnp.float32)
    coupling, weights = factor_parts(gram_matrix, cross_terms)
    projected = trailing - jnp.dot(panel_block.astype(jnp.float32), weights.astype(jnp.float32), precision=highest, preferred_element_type=jnp.float32)
    trailing_sketch = gauss_trail - jnp.dot(gauss_panel.astype(jnp.float32), weights.astype(jnp.float32), precision=highest, preferred_element_type=jnp.float32)
    return (sketch, coupling, projected, trailing_sketch)
```

```python
import functools

import jax
import jax.numpy as jnp
from jax import lax
from jax.experimental import pallas as pl
from jax.experimental.pallas import tpu as pltpu
from jax.sharding import PartitionSpec as P

MESH = pl.DeviceIdType.MESH
MOST = 64
PARTS = 4
F32 = jnp.float32
BF16 = jnp.bfloat16
NN = (((1,), (0,)), ((), ()))
NT = (((1,), (1,)), ((), ()))
TN = (((0,), (0,)), ((), ()))


def split(values):
    high = values.astype(BF16)
    return high, (values - high.astype(F32)).astype(BF16)


def dot(left, right, dims=NN):
    return lax.dot_general(left, right, dims, preferred_element_type=F32)


def dot3(left, right, dims=NN):
    return dot(left[0], right[0], dims) + (dot(left[0], right[1], dims) + dot(left[1], right[0], dims))


def full_dot(left, right, dims=NN):
    return lax.dot_general(left, right, dims, precision=lax.Precision.HIGHEST, preferred_element_type=F32)


def gather_and_sum(R, C, mat, gau, piv, trl, sketch_o, gtrail_o, gpan_o, sums_o, phi_o, plo_o,
                   gath, part1, part2, in1, in2, full, gpbuf,
                   g_send, g_recv, y_send, y_recv, f_send, f_recv, s1_send, s1_recv, s2_send, s2_recv,
                   a_send, a_recv, p_send, p_recv):
    r, c = lax.axis_index("rows"), lax.axis_index("cols")
    cols_dev, panel = mat.shape[1], piv.shape[1]
    share = gau.shape[0] // R
    psh = panel // R
    ny = C // 2
    y, k = c // 2, c % 2
    partner = c + 1 - 2 * k

    barrier = pltpu.get_barrier_semaphore()
    for d in range(1, C):
        pl.semaphore_signal(barrier, inc=1, device_id=(r, lax.rem(c + d, C)), device_id_type=MESH)
    for d in range(1, R):
        pl.semaphore_signal(barrier, inc=1, device_id=(lax.rem(r + d, R), c), device_id_type=MESH)

    prow = jnp.broadcast_to(piv[...], (panel, panel))
    pcol = jnp.transpose(prow.astype(F32)).astype(jnp.int32)
    brow = jnp.zeros_like(prow)
    bcol = jnp.zeros_like(prow)
    for b in range(1, C):
        brow += (prow >= b * cols_dev).astype(jnp.int32)
        bcol += (pcol >= b * cols_dev).astype(jnp.int32)
    sub = lax.broadcasted_iota(jnp.int32, (panel, panel), 0)
    lane = lax.broadcasted_iota(jnp.int32, (panel, panel), 1)
    same = brow == bcol
    rank_row = jnp.sum(jnp.where(same & (sub < lane), 1.0, 0.0), axis=0, keepdims=True)
    rank_col = jnp.sum(jnp.where(same & (lane < sub), 1.0, 0.0), axis=1, keepdims=True)
    slot_row = brow[:1, :] * MOST + rank_row.astype(jnp.int32)
    slot_col = bcol[:, :1] * MOST + rank_col.astype(jnp.int32)
    e1 = (slot_row - c * MOST == lax.broadcasted_iota(jnp.int32, (MOST, panel), 0)).astype(F32).astype(BF16)
    e2 = (pcol[:, :1] - c * cols_dev == lax.broadcasted_iota(jnp.int32, (panel, cols_dev), 1)).astype(F32).astype(BF16)
    sel = dot(e1, e2).astype(BF16)
    m2 = split(mat[...])
    gath[c] = dot(sel, m2[0], NT) + dot(sel, m2[1], NT)

    pl.semaphore_wait(barrier, C - 1 + R - 1)

    def block_copy(source, q, target, send, recv):
        piece = gath.at[source, pl.ds(q * (MOST // PARTS), MOST // PARTS)]
        return pltpu.make_async_remote_copy(piece, piece, send, recv, device_id=(r, target), device_id_type=MESH)

    waits = []
    across = {}
    for q in range(PARTS):
        for d in range(1, ny):
            cp = block_copy(c, q, lax.rem(y + d, ny) * 2 + k, y_send.at[d - 1, q], y_recv.at[d - 1, q])
            cp.start()
            across[d, q] = cp
    for q in range(PARTS):
        cp = block_copy(c, q, partner, g_send.at[q], g_recv.at[q])
        cp.start()
        waits.append(cp)

    g2 = split(gau[...])
    t2 = split(trl[...])
    part1[:, :cols_dev] = dot3(g2, m2)
    part1[:, cols_dev:] = dot3(g2, t2)

    def scatter(part, into, rows, send, recv):
        out = []
        for d in range(1, R):
            p = lax.rem(r + d, R)
            cp = pltpu.make_async_remote_copy(
                part.at[pl.ds(pl.multiple_of(p * rows, 8), rows)], into.at[d - 1], send.at[d - 1], recv.at[d - 1],
                device_id=(p, c), device_id_type=MESH)
            cp.start()
            out.append(cp)
        return out

    first = scatter(part1, in1, share, s1_send, s1_recv)

    relays = []
    for q in range(PARTS):
        for d in range(1, ny):
            across[d, q].wait_recv()
            source = lax.rem(y + ny - d, ny) * 2 + k
            cp = block_copy(source, q, partner, f_send.at[d - 1, q], f_recv.at[d - 1, q])
            cp.start()
            relays.append(cp)
    for cp in waits:
        cp.wait_recv()
    for cp in relays:
        cp.wait_recv()

    place = (slot_col == lax.broadcasted_iota(jnp.int32, (panel, C * MOST), 1)).astype(F32).astype(BF16)
    got = split(gath[...].reshape(C * MOST, gath.shape[2]))
    high = dot(place, got[0])
    low = dot(place, got[1])
    p2 = (high.astype(BF16), low.astype(BF16))
    hl = dot(p2[0], p2[1], NT)
    part2[:, :panel] = dot(p2[0], p2[0], NT) + (hl + jnp.transpose(hl))
    part2[:, panel:] = dot3(p2, t2)
    second = scatter(part2, in2, psh, s2_send, s2_recv)

    phi_o[...] = jnp.transpose(high).astype(BF16)
    plo_o[...] = jnp.transpose(low).astype(BF16)

    for cp in first:
        cp.wait_recv()
    total = part1[pl.ds(pl.multiple_of(r * share, 8), share)]
    for d in range(1, R):
        total += in1[d - 1]
    sketch_o[...] = total[:, :cols_dev]
    gtrail_o[...] = total[:, cols_dev:]
    e3 = (prow[:1, :] - c * cols_dev == lax.broadcasted_iota(jnp.int32, (cols_dev, panel), 0)).astype(F32)
    gpbuf[0] = full_dot(total[:, :cols_dev], e3)
    third = []
    for d in range(1, C):
        cp = pltpu.make_async_remote_copy(
            gpbuf.at[0], gpbuf.at[d], p_send.at[d - 1], p_recv.at[d - 1],
            device_id=(r, lax.rem(c + d, C)), device_id_type=MESH)
        cp.start()
        third.append(cp)

    for cp in second:
        cp.wait_recv()
    mine = pl.ds(pl.multiple_of(r * psh, 8), psh)
    total2 = part2[mine]
    for d in range(1, R):
        total2 += in2[d - 1]
    full[mine] = total2
    fourth = []
    for d in range(1, R):
        cp = pltpu.make_async_remote_copy(
            full.at[mine], full.at[mine], a_send.at[d - 1], a_recv.at[d - 1],
            device_id=(lax.rem(r + d, R), c), device_id_type=MESH)
        cp.start()
        fourth.append(cp)

    for cp in third:
        cp.wait_recv()
    gp = gpbuf[0]
    for d in range(1, C):
        gp += gpbuf[d]
    gpan_o[...] = gp
    for cp in fourth:
        cp.wait_recv()
    sums_o[...] = full[...]
    for cp in list(across.values()) + waits + relays + first + second + third + fourth:
        cp.wait_send()


def factor_inverse(a):
    n = a.shape[0]
    rows = lax.broadcasted_iota(jnp.int32, (8, n), 0)
    lanes = lax.broadcasted_iota(jnp.int32, (8, n), 1)
    left = [a[8 * b:8 * b + 8, :] for b in range(n // 8)]
    right = [jnp.where(lanes == rows + 8 * b, 1.0, 0.0) for b in range(n // 8)]
    for j in range(n):
        b0, s = j // 8, j % 8
        row = left[b0][s:s + 1, :]
        scale = 1.0 / row[:, j:j + 1]
        lrow = row * scale
        rrow = right[b0][s:s + 1, :] * scale
        for b in range(b0, n // 8):
            col = jnp.broadcast_to(left[b][:, j:j + 1], (8, n))
            if b == b0:
                col = jnp.where(rows > s, col, 0.0)
            left[b] = left[b] - col * lrow
            right[b] = right[b] - col * rrow
    out = []
    for b in range(n // 8):
        diag = jnp.sum(jnp.where(lanes == rows + 8 * b, left[b], 0.0), axis=1, keepdims=True)
        out.append(right[b] * lax.rsqrt(diag))
    return jnp.concatenate(out, axis=0)


def solve_and_project(sums, gtrail, gpan, phi, plo, trl, coupling_o, projected_o, tsk_o, hbuf, lbuf, tbuf, sems):
    copies = [pltpu.make_async_copy(a, b, sems.at[i])
              for i, (a, b) in enumerate(((phi, hbuf), (plo, lbuf), (trl, tbuf)))]
    for cp in copies:
        cp.start()
    n = sums.shape[0]
    h = n // 2
    c1, c2 = sums[:h, n:], sums[h:, n:]
    i1 = factor_inverse(sums[:h, :h])
    l21 = full_dot(sums[h:, :h], i1, NT)
    k1 = full_dot(i1, c1)
    i2 = factor_inverse(sums[h:, h:n] - full_dot(l21, l21, NT))
    k2 = full_dot(i2, c2 - full_dot(l21, k1))
    coupling_o[:h, :] = k1
    coupling_o[h:, :] = k2
    w2 = full_dot(jnp.transpose(i2), k2)
    w1 = full_dot(jnp.transpose(i1), k1 - full_dot(jnp.transpose(l21), w2))
    weights = jnp.concatenate([w1, w2], axis=0)
    tsk_o[...] = gtrail[...] - full_dot(gpan[...], weights)
    w = split(weights)
    for cp in copies:
        cp.wait()
    projected_o[...] = tbuf[...] - dot3((hbuf[...], lbuf[...]), w)


def shards(R, C, matrix, gaussian, pivots, trailing):
    depth, cols_dev = matrix.shape
    sketch_rows = gaussian.shape[0]
    panel = pivots.shape[0]
    slab = trailing.shape[1]
    share, psh = sketch_rows // R, panel // R
    ny = max(C // 2 - 1, 1)
    vm = pl.BlockSpec(memory_space=pltpu.VMEM)
    anywhere = pl.BlockSpec(memory_space=pl.ANY)
    dma = pltpu.SemaphoreType.DMA
    sketch, gtrail, gpan, sums, phi, plo = pl.pallas_call(
        functools.partial(gather_and_sum, R, C),
        out_shape=[
            jax.ShapeDtypeStruct((share, cols_dev), F32),
            jax.ShapeDtypeStruct((share, slab), F32),
            jax.ShapeDtypeStruct((share, panel), F32),
            jax.ShapeDtypeStruct((panel, panel + slab), F32),
            jax.ShapeDtypeStruct((depth, panel), BF16),
            jax.ShapeDtypeStruct((depth, panel), BF16),
        ],
        in_specs=[vm] * 4,
        out_specs=[vm] * 6,
        scratch_shapes=[
            pltpu.VMEM((C, MOST, depth), F32),
            pltpu.VMEM((sketch_rows, cols_dev + slab), F32),
            pltpu.VMEM((panel, panel + slab), F32),
            pltpu.VMEM((R - 1, share, cols_dev + slab), F32),
            pltpu.VMEM((R - 1, psh, panel + slab), F32),
            pltpu.VMEM((panel, panel + slab), F32),
            pltpu.VMEM((C, share, panel), F32),
            dma((PARTS,)), dma((PARTS,)),
            dma((ny, PARTS)), dma((ny, PARTS)),
            dma((ny, PARTS)), dma((ny, PARTS)),
            dma((R - 1,)), dma((R - 1,)),
            dma((R - 1,)), dma((R - 1,)),
            dma((R - 1,)), dma((R - 1,)),
            dma((C - 1,)), dma((C - 1,)),
        ],
        compiler_params=pltpu.CompilerParams(
            collective_id=0, has_side_effects=True, vmem_limit_bytes=56 * 1024 * 1024),
    )(matrix, gaussian, pivots.reshape(1, panel), trailing)
    coupling, projected, tsk = pl.pallas_call(
        solve_and_project,
        out_shape=[
            jax.ShapeDtypeStruct((panel, slab), F32),
            jax.ShapeDtypeStruct((depth, slab), F32),
            jax.ShapeDtypeStruct((share, slab), F32),
        ],
        in_specs=[vm] * 3 + [anywhere] * 3,
        out_specs=[vm] * 3,
        scratch_shapes=[
            pltpu.VMEM((depth, panel), BF16),
            pltpu.VMEM((depth, panel), BF16),
            pltpu.VMEM((depth, slab), F32),
            dma((3,)),
        ],
        compiler_params=pltpu.CompilerParams(vmem_limit_bytes=56 * 1024 * 1024),
    )(sums, gtrail, gpan, phi, plo, trailing)
    return sketch, coupling, projected, tsk


def solution(mesh):
    placed = (P("rows", "cols"), P(None, "rows"), P(), P("rows", "cols"))
    return jax.shard_map(
        functools.partial(shards, mesh.shape["rows"], mesh.shape["cols"]),
        mesh=mesh,
        in_specs=placed,
        out_specs=(P("rows", "cols"), P(None, "cols"), P("rows", "cols"), P("rows", "cols")),
        check_vma=False,
    )
```

```python
import functools

import jax
import jax.numpy as jnp
from jax import lax
from jax.experimental import pallas as pl
from jax.experimental.pallas import tpu as pltpu
from jax.sharding import PartitionSpec as P

MESH = pl.DeviceIdType.MESH
MOST = 64
PARTS = 4
F32 = jnp.float32
BF16 = jnp.bfloat16
NN = (((1,), (0,)), ((), ()))
NT = (((1,), (1,)), ((), ()))
TN = (((0,), (0,)), ((), ()))


def split(values):
    high = values.astype(BF16)
    return high, (values - high.astype(F32)).astype(BF16)


def dot(left, right, dims=NN):
    return lax.dot_general(left, right, dims, preferred_element_type=F32)


def dot3(left, right, dims=NN):
    return dot(left[0], right[0], dims) + (dot(left[0], right[1], dims) + dot(left[1], right[0], dims))


def full_dot(left, right, dims=NN):
    return lax.dot_general(left, right, dims, precision=lax.Precision.HIGHEST, preferred_element_type=F32)


def gather_and_sum(R, C, mat, gau, piv, trl, sketch_o, gtrail_o, gpan_o, sums_o, phi_o, plo_o,
                   gath, part1, part2, in1, in2, full, gpbuf,
                   g_send, g_recv, y_send, y_recv, f_send, f_recv, s1_send, s1_recv, s2_send, s2_recv,
                   a_send, a_recv, p_send, p_recv):
    r, c = lax.axis_index("rows"), lax.axis_index("cols")
    cols_dev, panel = mat.shape[1], piv.shape[1]
    share = gau.shape[0] // R
    psh = panel // R
    ny = C // 2
    y, k = c // 2, c % 2
    partner = c + 1 - 2 * k

    barrier = pltpu.get_barrier_semaphore()
    for d in range(1, C):
        pl.semaphore_signal(barrier, inc=1, device_id=(r, lax.rem(c + d, C)), device_id_type=MESH)
    for d in range(1, R):
        pl.semaphore_signal(barrier, inc=1, device_id=(lax.rem(r + d, R), c), device_id_type=MESH)

    prow = jnp.broadcast_to(piv[...], (panel, panel))
    pcol = jnp.transpose(prow.astype(F32)).astype(jnp.int32)
    brow = jnp.zeros_like(prow)
    bcol = jnp.zeros_like(prow)
    for b in range(1, C):
        brow += (prow >= b * cols_dev).astype(jnp.int32)
        bcol += (pcol >= b * cols_dev).astype(jnp.int32)
    sub = lax.broadcasted_iota(jnp.int32, (panel, panel), 0)
    lane = lax.broadcasted_iota(jnp.int32, (panel, panel), 1)
    same = brow == bcol
    rank_row = jnp.sum(jnp.where(same & (sub < lane), 1.0, 0.0), axis=0, keepdims=True)
    rank_col = jnp.sum(jnp.where(same & (lane < sub), 1.0, 0.0), axis=1, keepdims=True)
    slot_row = brow[:1, :] * MOST + rank_row.astype(jnp.int32)
    slot_col = bcol[:, :1] * MOST + rank_col.astype(jnp.int32)
    e1 = (slot_row - c * MOST == lax.broadcasted_iota(jnp.int32, (MOST, panel), 0)).astype(F32).astype(BF16)
    e2 = (pcol[:, :1] - c * cols_dev == lax.broadcasted_iota(jnp.int32, (panel, cols_dev), 1)).astype(F32).astype(BF16)
    sel = dot(e1, e2).astype(BF16)
    m2 = split(mat[...])
    gath[c] = dot(sel, m2[0], NT) + dot(sel, m2[1], NT)

    pl.semaphore_wait(barrier, C - 1 + R - 1)

    def block_copy(source, q, target, send, recv):
        piece = gath.at[source, pl.ds(q * (MOST // PARTS), MOST // PARTS)]
        return pltpu.make_async_remote_copy(piece, piece, send, recv, device_id=(r, target), device_id_type=MESH)

    waits = []
    across = {}
    for q in range(PARTS):
        for d in range(1, ny):
            cp = block_copy(c, q, lax.rem(y + d, ny) * 2 + k, y_send.at[d - 1, q], y_recv.at[d - 1, q])
            cp.start()
            across[d, q] = cp
    for q in range(PARTS):
        cp = block_copy(c, q, partner, g_send.at[q], g_recv.at[q])
        cp.start()
        waits.append(cp)

    g2 = split(gau[...])
    t2 = split(trl[...])
    part1[:, :cols_dev] = dot3(g2, m2)
    part1[:, cols_dev:] = dot3(g2, t2)

    def scatter(part, into, rows, send, recv):
        out = []
        for d in range(1, R):
            p = lax.rem(r + d, R)
            cp = pltpu.make_async_remote_copy(
                part.at[pl.ds(pl.multiple_of(p * rows, 8), rows)], into.at[d - 1], send.at[d - 1], recv.at[d - 1],
                device_id=(p, c), device_id_type=MESH)
            cp.start()
            out.append(cp)
        return out

    first = scatter(part1, in1, share, s1_send, s1_recv)

    relays = []
    for q in range(PARTS):
        for d in range(1, ny):
            across[d, q].wait_recv()
            source = lax.rem(y + ny - d, ny) * 2 + k
            cp = block_copy(source, q, partner, f_send.at[d - 1, q], f_recv.at[d - 1, q])
            cp.start()
            relays.append(cp)
    for cp in waits:
        cp.wait_recv()
    for cp in relays:
        cp.wait_recv()

    place = (slot_col == lax.broadcasted_iota(jnp.int32, (panel, C * MOST), 1)).astype(F32).astype(BF16)
    got = split(gath[...].reshape(C * MOST, gath.shape[2]))
    high = dot(place, got[0])
    low = dot(place, got[1])
    p2 = (high.astype(BF16), low.astype(BF16))
    hl = dot(p2[0], p2[1], NT)
    part2[:, :panel] = dot(p2[0], p2[0], NT) + (hl + jnp.transpose(hl))
    part2[:, panel:] = dot3(p2, t2)
    second = scatter(part2, in2, psh, s2_send, s2_recv)

    phi_o[...] = jnp.transpose(high).astype(BF16)
    plo_o[...] = jnp.transpose(low).astype(BF16)

    for cp in first:
        cp.wait_recv()
    total = part1[pl.ds(pl.multiple_of(r * share, 8), share)]
    for d in range(1, R):
        total += in1[d - 1]
    sketch_o[...] = total[:, :cols_dev]
    gtrail_o[...] = total[:, cols_dev:]
    e3 = (prow[:1, :] - c * cols_dev == lax.broadcasted_iota(jnp.int32, (cols_dev, panel), 0)).astype(F32)
    gpbuf[0] = full_dot(total[:, :cols_dev], e3)
    third = []
    for d in range(1, C):
        cp = pltpu.make_async_remote_copy(
            gpbuf.at[0], gpbuf.at[d], p_send.at[d - 1], p_recv.at[d - 1],
            device_id=(r, lax.rem(c + d, C)), device_id_type=MESH)
        cp.start()
        third.append(cp)

    for cp in second:
        cp.wait_recv()
    mine = pl.ds(pl.multiple_of(r * psh, 8), psh)
    total2 = part2[mine]
    for d in range(1, R):
        total2 += in2[d - 1]
    full[mine] = total2
    fourth = []
    for d in range(1, R):
        cp = pltpu.make_async_remote_copy(
            full.at[mine], full.at[mine], a_send.at[d - 1], a_recv.at[d - 1],
            device_id=(lax.rem(r + d, R), c), device_id_type=MESH)
        cp.start()
        fourth.append(cp)

    for cp in third:
        cp.wait_recv()
    gp = gpbuf[0]
    for d in range(1, C):
        gp += gpbuf[d]
    gpan_o[...] = gp
    for cp in fourth:
        cp.wait_recv()
    sums_o[...] = full[...]
    for cp in list(across.values()) + waits + relays + first + second + third + fourth:
        cp.wait_send()


def factor_inverse(a):
    n = a.shape[0]
    rows = lax.broadcasted_iota(jnp.int32, (8, n), 0)
    lanes = lax.broadcasted_iota(jnp.int32, (8, n), 1)
    left = [a[8 * b:8 * b + 8, :] for b in range(n // 8)]
    right = [jnp.where(lanes == rows + 8 * b, 1.0, 0.0) for b in range(n // 8)]
    out = []
    for b0 in range(n // 8):
        x, y = left[b0], right[b0]
        cols = [jnp.broadcast_to(x[:, 8 * b0 + i:8 * b0 + i + 1], (8, n)) for i in range(8)]
        done = []
        for s in range(0, 8, 2):
            c0, c1 = cols[s], cols[s + 1]
            p, q, t = c0[s:s + 1], c0[s + 1:s + 2], c1[s + 1:s + 2]
            det = p * t - q * q
            inv = 1.0 / det
            ip, iq, it = t * inv, -q * inv, p * inv
            y0, y1 = y[s:s + 1], y[s + 1:s + 2]
            done.append(y0 * lax.rsqrt(p))
            done.append((y1 - (q / p) * y0) * lax.rsqrt(det / p))

            def eliminate(block):
                r0, r1 = block[s:s + 1], block[s + 1:s + 2]
                u0, u1 = ip * r0 + iq * r1, iq * r0 + it * r1
                return jnp.where(rows == s, u0, jnp.where(rows == s + 1, u1, block - c0 * u0 - c1 * u1))

            for i in range(s + 2, 8):
                cols[i] = eliminate(cols[i])
            x, y = eliminate(x), eliminate(y)
        out.append(jnp.concatenate(done, axis=0))
        for b in range(b0 + 1, n // 8):
            across = [jnp.broadcast_to(left[b][:, 8 * b0 + i:8 * b0 + i + 1], (8, n)) for i in range(8)]
            for i in range(8):
                left[b] = left[b] - across[i] * x[i:i + 1]
                right[b] = right[b] - across[i] * y[i:i + 1]
    return jnp.concatenate(out, axis=0)


def solve_and_project(sums, gtrail, gpan, phi, plo, trl, coupling_o, projected_o, tsk_o, hbuf, lbuf, tbuf, sems):
    copies = [pltpu.make_async_copy(a, b, sems.at[i])
              for i, (a, b) in enumerate(((phi, hbuf), (plo, lbuf), (trl, tbuf)))]
    for cp in copies:
        cp.start()
    n = sums.shape[0]
    h = n // 2
    c1, c2 = sums[:h, n:], sums[h:, n:]
    i1 = factor_inverse(sums[:h, :h])
    l21 = full_dot(sums[h:, :h], i1, NT)
    k1 = full_dot(i1, c1)
    i2 = factor_inverse(sums[h:, h:n] - full_dot(l21, l21, NT))
    k2 = full_dot(i2, c2 - full_dot(l21, k1))
    coupling_o[:h, :] = k1
    coupling_o[h:, :] = k2
    w2 = full_dot(jnp.transpose(i2), k2)
    w1 = full_dot(jnp.transpose(i1), k1 - full_dot(jnp.transpose(l21), w2))
    weights = jnp.concatenate([w1, w2], axis=0)
    tsk_o[...] = gtrail[...] - full_dot(gpan[...], weights)
    w = split(weights)
    for cp in copies:
        cp.wait()
    projected_o[...] = tbuf[...] - dot3((hbuf[...], lbuf[...]), w)


def shards(R, C, matrix, gaussian, pivots, trailing):
    depth, cols_dev = matrix.shape
    sketch_rows = gaussian.shape[0]
    panel = pivots.shape[0]
    slab = trailing.shape[1]
    share, psh = sketch_rows // R, panel // R
    ny = max(C // 2 - 1, 1)
    vm = pl.BlockSpec(memory_space=pltpu.VMEM)
    anywhere = pl.BlockSpec(memory_space=pl.ANY)
    dma = pltpu.SemaphoreType.DMA
    sketch, gtrail, gpan, sums, phi, plo = pl.pallas_call(
        functools.partial(gather_and_sum, R, C),
        out_shape=[
            jax.ShapeDtypeStruct((share, cols_dev), F32),
            jax.ShapeDtypeStruct((share, slab), F32),
            jax.ShapeDtypeStruct((share, panel), F32),
            jax.ShapeDtypeStruct((panel, panel + slab), F32),
            jax.ShapeDtypeStruct((depth, panel), BF16),
            jax.ShapeDtypeStruct((depth, panel), BF16),
        ],
        in_specs=[vm] * 4,
        out_specs=[vm] * 6,
        scratch_shapes=[
            pltpu.VMEM((C, MOST, depth), F32),
            pltpu.VMEM((sketch_rows, cols_dev + slab), F32),
            pltpu.VMEM((panel, panel + slab), F32),
            pltpu.VMEM((R - 1, share, cols_dev + slab), F32),
            pltpu.VMEM((R - 1, psh, panel + slab), F32),
            pltpu.VMEM((panel, panel + slab), F32),
            pltpu.VMEM((C, share, panel), F32),
            dma((PARTS,)), dma((PARTS,)),
            dma((ny, PARTS)), dma((ny, PARTS)),
            dma((ny, PARTS)), dma((ny, PARTS)),
            dma((R - 1,)), dma((R - 1,)),
            dma((R - 1,)), dma((R - 1,)),
            dma((R - 1,)), dma((R - 1,)),
            dma((C - 1,)), dma((C - 1,)),
        ],
        compiler_params=pltpu.CompilerParams(
            collective_id=0, has_side_effects=True, vmem_limit_bytes=56 * 1024 * 1024),
    )(matrix, gaussian, pivots.reshape(1, panel), trailing)
    coupling, projected, tsk = pl.pallas_call(
        solve_and_project,
        out_shape=[
            jax.ShapeDtypeStruct((panel, slab), F32),
            jax.ShapeDtypeStruct((depth, slab), F32),
            jax.ShapeDtypeStruct((share, slab), F32),
        ],
        in_specs=[vm] * 3 + [anywhere] * 3,
        out_specs=[vm] * 3,
        scratch_shapes=[
            pltpu.VMEM((depth, panel), BF16),
            pltpu.VMEM((depth, panel), BF16),
            pltpu.VMEM((depth, slab), F32),
            dma((3,)),
        ],
        compiler_params=pltpu.CompilerParams(vmem_limit_bytes=56 * 1024 * 1024),
    )(sums, gtrail, gpan, phi, plo, trailing)
    return sketch, coupling, projected, tsk


def solution(mesh):
    placed = (P("rows", "cols"), P(None, "rows"), P(), P("rows", "cols"))
    return jax.shard_map(
        functools.partial(shards, mesh.shape["rows"], mesh.shape["cols"]),
        mesh=mesh,
        in_specs=placed,
        out_specs=(P("rows", "cols"), P(None, "cols"), P("rows", "cols"), P("rows", "cols")),
        check_vma=False,
    )
```

```python
import functools

import jax
import jax.numpy as jnp
from jax import lax
from jax.experimental import pallas as pl
from jax.experimental.pallas import tpu as pltpu
from jax.sharding import PartitionSpec as P

MESH = pl.DeviceIdType.MESH
MOST = 64
PARTS = 4
F32 = jnp.float32
BF16 = jnp.bfloat16
NN = (((1,), (0,)), ((), ()))
NT = (((1,), (1,)), ((), ()))
TN = (((0,), (0,)), ((), ()))


def split(values):
    high = values.astype(BF16)
    return high, (values - high.astype(F32)).astype(BF16)


def dot(left, right, dims=NN):
    return lax.dot_general(left, right, dims, preferred_element_type=F32)


def dot3(left, right, dims=NN):
    return dot(left[0], right[0], dims) + (dot(left[0], right[1], dims) + dot(left[1], right[0], dims))


def full_dot(left, right, dims=NN):
    return lax.dot_general(left, right, dims, precision=lax.Precision.HIGHEST, preferred_element_type=F32)


def gather_and_sum(R, C, mat, gau, piv, trl, sketch_o, gtrail_o, gpan_o, sums_o, phi_o, plo_o,
                   gath, part1, part2, in1, in2, full, gpbuf,
                   g_send, g_recv, y_send, y_recv, f_send, f_recv, s1_send, s1_recv, s2_send, s2_recv,
                   a_send, a_recv, p_send, p_recv):
    r, c = lax.axis_index("rows"), lax.axis_index("cols")
    cols_dev, panel = mat.shape[1], piv.shape[1]
    share = gau.shape[0] // R
    psh = panel // R
    ny = C // 2
    y, k = c // 2, c % 2
    partner = c + 1 - 2 * k

    barrier = pltpu.get_barrier_semaphore()
    for d in range(1, C):
        pl.semaphore_signal(barrier, inc=1, device_id=(r, lax.rem(c + d, C)), device_id_type=MESH)
    for d in range(1, R):
        pl.semaphore_signal(barrier, inc=1, device_id=(lax.rem(r + d, R), c), device_id_type=MESH)

    prow = jnp.broadcast_to(piv[...], (panel, panel))
    pcol = jnp.transpose(prow.astype(F32)).astype(jnp.int32)
    brow = jnp.zeros_like(prow)
    bcol = jnp.zeros_like(prow)
    for b in range(1, C):
        brow += (prow >= b * cols_dev).astype(jnp.int32)
        bcol += (pcol >= b * cols_dev).astype(jnp.int32)
    sub = lax.broadcasted_iota(jnp.int32, (panel, panel), 0)
    lane = lax.broadcasted_iota(jnp.int32, (panel, panel), 1)
    same = brow == bcol
    rank_row = jnp.sum(jnp.where(same & (sub < lane), 1.0, 0.0), axis=0, keepdims=True)
    rank_col = jnp.sum(jnp.where(same & (lane < sub), 1.0, 0.0), axis=1, keepdims=True)
    slot_row = brow[:1, :] * MOST + rank_row.astype(jnp.int32)
    slot_col = bcol[:, :1] * MOST + rank_col.astype(jnp.int32)
    e1 = (slot_row - c * MOST == lax.broadcasted_iota(jnp.int32, (MOST, panel), 0)).astype(F32).astype(BF16)
    e2 = (pcol[:, :1] - c * cols_dev == lax.broadcasted_iota(jnp.int32, (panel, cols_dev), 1)).astype(F32).astype(BF16)
    sel = dot(e1, e2).astype(BF16)
    m2 = split(mat[...])
    gath[c] = dot(sel, m2[0], NT) + dot(sel, m2[1], NT)

    pl.semaphore_wait(barrier, C - 1 + R - 1)

    def block_copy(source, q, target, send, recv):
        piece = gath.at[source, pl.ds(q * (MOST // PARTS), MOST // PARTS)]
        return pltpu.make_async_remote_copy(piece, piece, send, recv, device_id=(r, target), device_id_type=MESH)

    waits = []
    across = {}
    for q in range(PARTS):
        for d in range(1, ny):
            cp = block_copy(c, q, lax.rem(y + d, ny) * 2 + k, y_send.at[d - 1, q], y_recv.at[d - 1, q])
            cp.start()
            across[d, q] = cp
    for q in range(PARTS):
        cp = block_copy(c, q, partner, g_send.at[q], g_recv.at[q])
        cp.start()
        waits.append(cp)

    g2 = split(gau[...])
    t2 = split(trl[...])
    part1[:, :cols_dev] = dot3(g2, m2)
    part1[:, cols_dev:] = dot3(g2, t2)

    def scatter(part, into, rows, send, recv):
        out = []
        for d in range(1, R):
            p = lax.rem(r + d, R)
            cp = pltpu.make_async_remote_copy(
                part.at[pl.ds(pl.multiple_of(p * rows, 8), rows)], into.at[d - 1], send.at[d - 1], recv.at[d - 1],
                device_id=(p, c), device_id_type=MESH)
            cp.start()
            out.append(cp)
        return out

    first = scatter(part1, in1, share, s1_send, s1_recv)

    relays = []
    for q in range(PARTS):
        for d in range(1, ny):
            across[d, q].wait_recv()
            source = lax.rem(y + ny - d, ny) * 2 + k
            cp = block_copy(source, q, partner, f_send.at[d - 1, q], f_recv.at[d - 1, q])
            cp.start()
            relays.append(cp)
    for cp in waits:
        cp.wait_recv()
    for cp in relays:
        cp.wait_recv()

    place = (slot_col == lax.broadcasted_iota(jnp.int32, (panel, C * MOST), 1)).astype(F32).astype(BF16)
    got = split(gath[...].reshape(C * MOST, gath.shape[2]))
    high = dot(place, got[0])
    low = dot(place, got[1])
    p2 = (high.astype(BF16), low.astype(BF16))
    hl = dot(p2[0], p2[1], NT)
    part2[:, :panel] = dot(p2[0], p2[0], NT) + (hl + jnp.transpose(hl))
    part2[:, panel:] = dot3(p2, t2)
    second = scatter(part2, in2, psh, s2_send, s2_recv)

    phi_o[...] = jnp.transpose(high).astype(BF16)
    plo_o[...] = jnp.transpose(low).astype(BF16)

    for cp in first:
        cp.wait_recv()
    total = part1[pl.ds(pl.multiple_of(r * share, 8), share)]
    for d in range(1, R):
        total += in1[d - 1]
    sketch_o[...] = total[:, :cols_dev]
    gtrail_o[...] = total[:, cols_dev:]
    e3 = (prow[:1, :] - c * cols_dev == lax.broadcasted_iota(jnp.int32, (cols_dev, panel), 0)).astype(F32)
    gpbuf[0] = full_dot(total[:, :cols_dev], e3)
    third = []
    for d in range(1, C):
        cp = pltpu.make_async_remote_copy(
            gpbuf.at[0], gpbuf.at[d], p_send.at[d - 1], p_recv.at[d - 1],
            device_id=(r, lax.rem(c + d, C)), device_id_type=MESH)
        cp.start()
        third.append(cp)

    for cp in second:
        cp.wait_recv()
    mine = pl.ds(pl.multiple_of(r * psh, 8), psh)
    total2 = part2[mine]
    for d in range(1, R):
        total2 += in2[d - 1]
    full[mine] = total2
    fourth = []
    for d in range(1, R):
        cp = pltpu.make_async_remote_copy(
            full.at[mine], full.at[mine], a_send.at[d - 1], a_recv.at[d - 1],
            device_id=(lax.rem(r + d, R), c), device_id_type=MESH)
        cp.start()
        fourth.append(cp)

    for cp in third:
        cp.wait_recv()
    gp = gpbuf[0]
    for d in range(1, C):
        gp += gpbuf[d]
    gpan_o[...] = gp
    for cp in fourth:
        cp.wait_recv()
    sums_o[...] = full[...]
    for cp in list(across.values()) + waits + relays + first + second + third + fourth:
        cp.wait_send()


def ordered(place, values):
    high = values.astype(BF16)
    rest = values - high.astype(F32)
    mid = rest.astype(BF16)
    low = (rest - mid.astype(F32)).astype(BF16)
    return (dot(place, low) + dot(place, mid)) + dot(place, high)


def gather_by_halves(R, C, mat, gau_in, piv, trl_in, sketch_o, gtrail_o, gpan_o, sums_o, phi_o, plo_o, place_o,
                     gau, trl, gath, part1, near, far, in1, in_near, in_far, full_near, full_far, diag, gpbuf,
                     l_sem, g_send, g_recv, y_send, y_recv, f_send, f_recv, s_send, s_recv, n_send, n_recv,
                     o_send, o_recv, an_send, an_recv, ao_send, ao_recv, p_send, p_recv, d_send, d_recv):
    r, c = lax.axis_index("rows"), lax.axis_index("cols")
    cols_dev, panel = mat.shape[1], piv.shape[1]
    depth = mat.shape[0]
    share = gau.shape[0] // R
    half = panel // 2
    hsh = half // R
    y, k = c // 2, c % 2
    partner = c + 1 - 2 * k
    opposite = lax.rem(c + 2, C)

    loads = [pltpu.make_async_copy(trl_in, trl, l_sem.at[0]), pltpu.make_async_copy(gau_in, gau, l_sem.at[1])]
    for cp in loads:
        cp.start()
    barrier = pltpu.get_barrier_semaphore()
    for d in range(1, C):
        pl.semaphore_signal(barrier, inc=1, device_id=(r, lax.rem(c + d, C)), device_id_type=MESH)
    for d in range(1, R):
        pl.semaphore_signal(barrier, inc=1, device_id=(lax.rem(r + d, R), c), device_id_type=MESH)

    prow = jnp.broadcast_to(piv[...], (panel, panel))
    pcol = jnp.transpose(prow.astype(F32)).astype(jnp.int32)
    brow = jnp.zeros_like(prow)
    bcol = jnp.zeros_like(prow)
    for b in range(1, C):
        brow += (prow >= b * cols_dev).astype(jnp.int32)
        bcol += (pcol >= b * cols_dev).astype(jnp.int32)
    sub = lax.broadcasted_iota(jnp.int32, (panel, panel), 0)
    lane = lax.broadcasted_iota(jnp.int32, (panel, panel), 1)
    same = brow == bcol
    rank_row = jnp.sum(jnp.where(same & (sub < lane), 1.0, 0.0), axis=0, keepdims=True)
    rank_col = jnp.sum(jnp.where(same & (lane < sub), 1.0, 0.0), axis=1, keepdims=True)
    slot_row = brow[:1, :] * MOST + rank_row.astype(jnp.int32)
    slot_col = bcol[:, :1] * MOST + rank_col.astype(jnp.int32)
    e1 = (slot_row - c * MOST == lax.broadcasted_iota(jnp.int32, (MOST, panel), 0)).astype(F32).astype(BF16)
    e2 = (pcol[:, :1] - c * cols_dev == lax.broadcasted_iota(jnp.int32, (panel, cols_dev), 1)).astype(F32).astype(BF16)
    sel = dot(e1, e2).astype(BF16)
    m2 = split(mat[...])
    gath[c] = dot(sel, m2[0], NT) + dot(sel, m2[1], NT)

    pl.semaphore_wait(barrier, C - 1 + R - 1)

    def block_copy(source, q, target, send, recv):
        piece = gath.at[source, pl.ds(q * (MOST // PARTS), MOST // PARTS)]
        return pltpu.make_async_remote_copy(piece, piece, send, recv, device_id=(r, target), device_id_type=MESH)

    def scatter(part, into, rows, send, recv):
        out = []
        for d in range(1, R):
            p = lax.rem(r + d, R)
            cp = pltpu.make_async_remote_copy(
                part.at[pl.ds(pl.multiple_of(p * rows, 8), rows)], into.at[d - 1], send.at[d - 1], recv.at[d - 1],
                device_id=(p, c), device_id_type=MESH)
            cp.start()
            out.append(cp)
        return out

    def finish(copies, part, into, rows):
        for cp in copies:
            cp.wait_recv()
        total = part[pl.ds(pl.multiple_of(r * rows, 8), rows)]
        for d in range(1, R):
            total += into[d - 1]
        return total

    def spread(total, whole, rows, send, recv):
        mine = pl.ds(pl.multiple_of(r * rows, 8), rows)
        whole[mine] = total
        out = []
        for d in range(1, R):
            cp = pltpu.make_async_remote_copy(
                whole.at[mine], whole.at[mine], send.at[d - 1], recv.at[d - 1],
                device_id=(lax.rem(r + d, R), c), device_id_type=MESH)
            cp.start()
            out.append(cp)
        return out

    across = [block_copy(c, q, opposite, y_send.at[q], y_recv.at[q]) for q in range(PARTS)]
    beside = [block_copy(c, q, partner, g_send.at[q], g_recv.at[q]) for q in range(PARTS)]
    relays = [block_copy(opposite, q, partner, f_send.at[q], f_recv.at[q]) for q in range(PARTS)]
    for cp in across + beside:
        cp.start()

    loads[0].wait()
    t2 = split(trl[...])
    for cp in beside:
        cp.wait_recv()
    own = gath[pl.ds(2 * y, 2)].reshape(half, depth)
    o2 = split(own)
    near[:, :half] = dot3(o2, o2, NT)
    near[:, half:] = dot3(o2, t2)
    near_out = scatter(near, in_near, hsh, n_send, n_recv)

    loads[1].wait()
    g2 = split(gau[...])
    part1[:, :cols_dev] = dot3(g2, m2)
    part1[:, cols_dev:] = dot3(g2, t2)
    sketch_out = scatter(part1, in1, share, s_send, s_recv)

    near_all = spread(finish(near_out, near, in_near, hsh), full_near, hsh, an_send, an_recv)
    for q in range(PARTS):
        across[q].wait_recv()
        relays[q].start()
    own_t = jnp.transpose(own)
    t_high, t_low = split(own_t)
    phi_o[:, :half] = t_high
    plo_o[:, :half] = t_low
    for cp in near_all:
        cp.wait_recv()
    swap = pltpu.make_async_remote_copy(
        full_near.at[:, pl.ds(0, half)], diag, d_send.at[0], d_recv.at[0],
        device_id=(r, opposite), device_id_type=MESH)
    swap.start()
    for cp in relays:
        cp.wait_recv()

    other = gath[pl.ds(2 * (1 - y), 2)].reshape(half, depth)
    r2 = split(other)
    far[:, :half] = dot3(r2, o2, NT)
    far[:, half:] = dot3(r2, t2)
    far_out = scatter(far, in_far, hsh, o_send, o_recv)

    r_high, r_low = split(jnp.transpose(other))
    phi_o[:, half:] = r_high
    plo_o[:, half:] = r_low
    slot = lane + half * y
    slot = jnp.where(slot >= panel, slot - panel, slot)
    place = (slot_col == slot).astype(F32).astype(BF16)
    place_o[...] = place

    far_all = spread(finish(far_out, far, in_far, hsh), full_far, hsh, ao_send, ao_recv)

    total = finish(sketch_out, part1, in1, share)
    sketch_o[...] = total[:, :cols_dev]
    gtrail_o[...] = total[:, cols_dev:]
    e3 = (prow[:1, :] - c * cols_dev == lax.broadcasted_iota(jnp.int32, (cols_dev, panel), 0)).astype(F32)
    gpbuf[0] = full_dot(total[:, :cols_dev], e3)
    third = []
    for d in range(1, C):
        cp = pltpu.make_async_remote_copy(
            gpbuf.at[0], gpbuf.at[d], p_send.at[d - 1], p_recv.at[d - 1],
            device_id=(r, lax.rem(c + d, C)), device_id_type=MESH)
        cp.start()
        third.append(cp)
    swap.wait_recv()
    for cp in far_all:
        cp.wait_recv()
    mixed = full_far[:, :half]
    first_rows = jnp.concatenate([full_near[:, :half], jnp.transpose(mixed), full_near[:, half:]], axis=1)
    last_rows = jnp.concatenate([mixed, diag[...], full_far[:, half:]], axis=1)
    by_rows = ordered(place, jnp.concatenate([first_rows, last_rows], axis=0))
    sums_o[:, panel:] = by_rows[:, panel:]
    sums_o[:, :panel] = ordered(place, jnp.transpose(by_rows[:, :panel]))
    for cp in third:
        cp.wait_recv()
    gp = gpbuf[0]
    for d in range(1, C):
        gp += gpbuf[d]
    gpan_o[...] = gp
    for cp in across + beside + relays + near_out + sketch_out + near_all + far_out + far_all + third + [swap]:
        cp.wait_send()


def factor_inverse(a):
    n = a.shape[0]
    rows = lax.broadcasted_iota(jnp.int32, (8, n), 0)
    lanes = lax.broadcasted_iota(jnp.int32, (8, n), 1)
    left = [a[8 * b:8 * b + 8, :] for b in range(n // 8)]
    right = [jnp.where(lanes == rows + 8 * b, 1.0, 0.0) for b in range(n // 8)]
    out = []
    for b0 in range(n // 8):
        x, y = left[b0], right[b0]
        cols = [jnp.broadcast_to(x[:, 8 * b0 + i:8 * b0 + i + 1], (8, n)) for i in range(8)]
        done = []
        for s in range(0, 8, 2):
            c0, c1 = cols[s], cols[s + 1]
            p, q, t = c0[s:s + 1], c0[s + 1:s + 2], c1[s + 1:s + 2]
            det = p * t - q * q
            inv = 1.0 / det
            ip, iq, it = t * inv, -q * inv, p * inv
            y0, y1 = y[s:s + 1], y[s + 1:s + 2]
            done.append(y0 * lax.rsqrt(p))
            done.append((y1 - (q / p) * y0) * lax.rsqrt(det / p))

            def eliminate(block):
                r0, r1 = block[s:s + 1], block[s + 1:s + 2]
                u0, u1 = ip * r0 + iq * r1, iq * r0 + it * r1
                return jnp.where(rows == s, u0, jnp.where(rows == s + 1, u1, block - c0 * u0 - c1 * u1))

            for i in range(s + 2, 8):
                cols[i] = eliminate(cols[i])
            x, y = eliminate(x), eliminate(y)
        out.append(jnp.concatenate(done, axis=0))
        for b in range(b0 + 1, n // 8):
            across = [jnp.broadcast_to(left[b][:, 8 * b0 + i:8 * b0 + i + 1], (8, n)) for i in range(8)]
            for i in range(8):
                left[b] = left[b] - across[i] * x[i:i + 1]
                right[b] = right[b] - across[i] * y[i:i + 1]
    return jnp.concatenate(out, axis=0)


def solve_and_project(sums, gtrail, gpan, place, phi, plo, trl, coupling_o, projected_o, tsk_o, hbuf, lbuf, tbuf, sems):
    copies = [pltpu.make_async_copy(a, b, sems.at[i])
              for i, (a, b) in enumerate(((phi, hbuf), (plo, lbuf), (trl, tbuf)))]
    for cp in copies:
        cp.start()
    n = sums.shape[0]
    h = n // 2
    c1, c2 = sums[:h, n:], sums[h:, n:]
    i1 = factor_inverse(sums[:h, :h])
    l21 = full_dot(sums[h:, :h], i1, NT)
    k1 = full_dot(i1, c1)
    i2 = factor_inverse(sums[h:, h:n] - full_dot(l21, l21, NT))
    k2 = full_dot(i2, c2 - full_dot(l21, k1))
    coupling_o[:h, :] = k1
    coupling_o[h:, :] = k2
    w2 = full_dot(jnp.transpose(i2), k2)
    w1 = full_dot(jnp.transpose(i1), k1 - full_dot(jnp.transpose(l21), w2))
    weights = jnp.concatenate([w1, w2], axis=0)
    tsk_o[...] = gtrail[...] - full_dot(gpan[...], weights)
    w = tuple(dot(place[...], piece, TN).astype(BF16) for piece in split(weights))
    for cp in copies:
        cp.wait()
    projected_o[...] = tbuf[...] - dot3((hbuf[...], lbuf[...]), w)


def shards(R, C, matrix, gaussian, pivots, trailing):
    depth, cols_dev = matrix.shape
    sketch_rows = gaussian.shape[0]
    panel = pivots.shape[0]
    slab = trailing.shape[1]
    share, psh = sketch_rows // R, panel // R
    ny = max(C // 2 - 1, 1)
    vm = pl.BlockSpec(memory_space=pltpu.VMEM)
    anywhere = pl.BlockSpec(memory_space=pl.ANY)
    dma = pltpu.SemaphoreType.DMA
    if C == 4 and C * MOST == panel and panel == 2 * slab and (panel // 2) % (8 * R) == 0:
        half = panel // 2
        sketch, gtrail, gpan, sums, phi, plo, place = pl.pallas_call(
            functools.partial(gather_by_halves, R, C),
            out_shape=[
                jax.ShapeDtypeStruct((share, cols_dev), F32),
                jax.ShapeDtypeStruct((share, slab), F32),
                jax.ShapeDtypeStruct((share, panel), F32),
                jax.ShapeDtypeStruct((panel, panel + slab), F32),
                jax.ShapeDtypeStruct((depth, panel), BF16),
                jax.ShapeDtypeStruct((depth, panel), BF16),
                jax.ShapeDtypeStruct((panel, panel), BF16),
            ],
            in_specs=[vm, anywhere, vm, anywhere],
            out_specs=[vm] * 7,
            scratch_shapes=[
                pltpu.VMEM((sketch_rows, depth), F32),
                pltpu.VMEM((depth, slab), F32),
                pltpu.VMEM((C, MOST, depth), F32),
                pltpu.VMEM((sketch_rows, cols_dev + slab), F32),
                pltpu.VMEM((half, half + slab), F32),
                pltpu.VMEM((half, half + slab), F32),
                pltpu.VMEM((R - 1, share, cols_dev + slab), F32),
                pltpu.VMEM((R - 1, half // R, half + slab), F32),
                pltpu.VMEM((R - 1, half // R, half + slab), F32),
                pltpu.VMEM((half, half + slab), F32),
                pltpu.VMEM((half, half + slab), F32),
                pltpu.VMEM((half, half), F32),
                pltpu.VMEM((C, share, panel), F32),
                dma((2,)),
                *[dma((PARTS,))] * 6,
                *[dma((R - 1,))] * 10,
                *[dma((C - 1,))] * 2,
                *[dma((1,))] * 2,
            ],
            compiler_params=pltpu.CompilerParams(
                collective_id=0, has_side_effects=True, vmem_limit_bytes=56 * 1024 * 1024),
        )(matrix, gaussian, pivots.reshape(1, panel), trailing)
    else:
        sketch, gtrail, gpan, sums, phi, plo = pl.pallas_call(
            functools.partial(gather_and_sum, R, C),
            out_shape=[
                jax.ShapeDtypeStruct((share, cols_dev), F32),
                jax.ShapeDtypeStruct((share, slab), F32),
                jax.ShapeDtypeStruct((share, panel), F32),
                jax.ShapeDtypeStruct((panel, panel + slab), F32),
                jax.ShapeDtypeStruct((depth, panel), BF16),
                jax.ShapeDtypeStruct((depth, panel), BF16),
            ],
            in_specs=[vm] * 4,
            out_specs=[vm] * 6,
            scratch_shapes=[
                pltpu.VMEM((C, MOST, depth), F32),
                pltpu.VMEM((sketch_rows, cols_dev + slab), F32),
                pltpu.VMEM((panel, panel + slab), F32),
                pltpu.VMEM((R - 1, share, cols_dev + slab), F32),
                pltpu.VMEM((R - 1, psh, panel + slab), F32),
                pltpu.VMEM((panel, panel + slab), F32),
                pltpu.VMEM((C, share, panel), F32),
                dma((PARTS,)), dma((PARTS,)),
                dma((ny, PARTS)), dma((ny, PARTS)),
                dma((ny, PARTS)), dma((ny, PARTS)),
                dma((R - 1,)), dma((R - 1,)),
                dma((R - 1,)), dma((R - 1,)),
                dma((R - 1,)), dma((R - 1,)),
                dma((C - 1,)), dma((C - 1,)),
            ],
            compiler_params=pltpu.CompilerParams(
                collective_id=0, has_side_effects=True, vmem_limit_bytes=56 * 1024 * 1024),
        )(matrix, gaussian, pivots.reshape(1, panel), trailing)
        place = jnp.eye(panel, dtype=BF16)
    coupling, projected, tsk = pl.pallas_call(
        solve_and_project,
        out_shape=[
            jax.ShapeDtypeStruct((panel, slab), F32),
            jax.ShapeDtypeStruct((depth, slab), F32),
            jax.ShapeDtypeStruct((share, slab), F32),
        ],
        in_specs=[vm] * 4 + [anywhere] * 3,
        out_specs=[vm] * 3,
        scratch_shapes=[
            pltpu.VMEM((depth, panel), BF16),
            pltpu.VMEM((depth, panel), BF16),
            pltpu.VMEM((depth, slab), F32),
            dma((3,)),
        ],
        compiler_params=pltpu.CompilerParams(vmem_limit_bytes=56 * 1024 * 1024),
    )(sums, gtrail, gpan, place, phi, plo, trailing)
    return sketch, coupling, projected, tsk


def solution(mesh):
    placed = (P("rows", "cols"), P(None, "rows"), P(), P("rows", "cols"))
    return jax.shard_map(
        functools.partial(shards, mesh.shape["rows"], mesh.shape["cols"]),
        mesh=mesh,
        in_specs=placed,
        out_specs=(P("rows", "cols"), P(None, "cols"), P("rows", "cols"), P("rows", "cols")),
        check_vma=False,
    )
```

```python
import functools

import jax
import jax.numpy as jnp
from jax import lax
from jax.experimental import pallas as pl
from jax.experimental.pallas import tpu as pltpu
from jax.sharding import PartitionSpec as P

MESH = pl.DeviceIdType.MESH
MOST = 64
PARTS = 4
F32 = jnp.float32
BF16 = jnp.bfloat16
NN = (((1,), (0,)), ((), ()))
NT = (((1,), (1,)), ((), ()))
TN = (((0,), (0,)), ((), ()))


def split(values):
    high = values.astype(BF16)
    return high, (values - high.astype(F32)).astype(BF16)


def dot(left, right, dims=NN):
    return lax.dot_general(left, right, dims, preferred_element_type=F32)


def dot3(left, right, dims=NN):
    return dot(left[0], right[0], dims) + (dot(left[0], right[1], dims) + dot(left[1], right[0], dims))


def full_dot(left, right, dims=NN):
    return lax.dot_general(left, right, dims, precision=lax.Precision.HIGHEST, preferred_element_type=F32)


def gather_and_sum(R, C, mat, gau, piv, trl, sketch_o, gtrail_o, gpan_o, sums_o, phi_o, plo_o,
                   gath, part1, part2, in1, in2, full, gpbuf,
                   g_send, g_recv, y_send, y_recv, f_send, f_recv, s1_send, s1_recv, s2_send, s2_recv,
                   a_send, a_recv, p_send, p_recv):
    r, c = lax.axis_index("rows"), lax.axis_index("cols")
    cols_dev, panel = mat.shape[1], piv.shape[1]
    share = gau.shape[0] // R
    psh = panel // R
    ny = C // 2
    y, k = c // 2, c % 2
    partner = c + 1 - 2 * k

    barrier = pltpu.get_barrier_semaphore()
    for d in range(1, C):
        pl.semaphore_signal(barrier, inc=1, device_id=(r, lax.rem(c + d, C)), device_id_type=MESH)
    for d in range(1, R):
        pl.semaphore_signal(barrier, inc=1, device_id=(lax.rem(r + d, R), c), device_id_type=MESH)

    prow = jnp.broadcast_to(piv[...], (panel, panel))
    pcol = jnp.transpose(prow.astype(F32)).astype(jnp.int32)
    brow = jnp.zeros_like(prow)
    bcol = jnp.zeros_like(prow)
    for b in range(1, C):
        brow += (prow >= b * cols_dev).astype(jnp.int32)
        bcol += (pcol >= b * cols_dev).astype(jnp.int32)
    sub = lax.broadcasted_iota(jnp.int32, (panel, panel), 0)
    lane = lax.broadcasted_iota(jnp.int32, (panel, panel), 1)
    same = brow == bcol
    rank_row = jnp.sum(jnp.where(same & (sub < lane), 1.0, 0.0), axis=0, keepdims=True)
    rank_col = jnp.sum(jnp.where(same & (lane < sub), 1.0, 0.0), axis=1, keepdims=True)
    slot_row = brow[:1, :] * MOST + rank_row.astype(jnp.int32)
    slot_col = bcol[:, :1] * MOST + rank_col.astype(jnp.int32)
    e1 = (slot_row - c * MOST == lax.broadcasted_iota(jnp.int32, (MOST, panel), 0)).astype(F32).astype(BF16)
    e2 = (pcol[:, :1] - c * cols_dev == lax.broadcasted_iota(jnp.int32, (panel, cols_dev), 1)).astype(F32).astype(BF16)
    sel = dot(e1, e2).astype(BF16)
    m2 = split(mat[...])
    gath[c] = dot(sel, m2[0], NT) + dot(sel, m2[1], NT)

    pl.semaphore_wait(barrier, C - 1 + R - 1)

    def block_copy(source, q, target, send, recv):
        piece = gath.at[source, pl.ds(q * (MOST // PARTS), MOST // PARTS)]
        return pltpu.make_async_remote_copy(piece, piece, send, recv, device_id=(r, target), device_id_type=MESH)

    waits = []
    across = {}
    for q in range(PARTS):
        for d in range(1, ny):
            cp = block_copy(c, q, lax.rem(y + d, ny) * 2 + k, y_send.at[d - 1, q], y_recv.at[d - 1, q])
            cp.start()
            across[d, q] = cp
    for q in range(PARTS):
        cp = block_copy(c, q, partner, g_send.at[q], g_recv.at[q])
        cp.start()
        waits.append(cp)

    g2 = split(gau[...])
    t2 = split(trl[...])
    part1[:, :cols_dev] = dot3(g2, m2)
    part1[:, cols_dev:] = dot3(g2, t2)

    def scatter(part, into, rows, send, recv):
        out = []
        for d in range(1, R):
            p = lax.rem(r + d, R)
            cp = pltpu.make_async_remote_copy(
                part.at[pl.ds(pl.multiple_of(p * rows, 8), rows)], into.at[d - 1], send.at[d - 1], recv.at[d - 1],
                device_id=(p, c), device_id_type=MESH)
            cp.start()
            out.append(cp)
        return out

    first = scatter(part1, in1, share, s1_send, s1_recv)

    relays = []
    for q in range(PARTS):
        for d in range(1, ny):
            across[d, q].wait_recv()
            source = lax.rem(y + ny - d, ny) * 2 + k
            cp = block_copy(source, q, partner, f_send.at[d - 1, q], f_recv.at[d - 1, q])
            cp.start()
            relays.append(cp)
    for cp in waits:
        cp.wait_recv()
    for cp in relays:
        cp.wait_recv()

    place = (slot_col == lax.broadcasted_iota(jnp.int32, (panel, C * MOST), 1)).astype(F32).astype(BF16)
    got = split(gath[...].reshape(C * MOST, gath.shape[2]))
    high = dot(place, got[0])
    low = dot(place, got[1])
    p2 = (high.astype(BF16), low.astype(BF16))
    hl = dot(p2[0], p2[1], NT)
    part2[:, :panel] = dot(p2[0], p2[0], NT) + (hl + jnp.transpose(hl))
    part2[:, panel:] = dot3(p2, t2)
    second = scatter(part2, in2, psh, s2_send, s2_recv)

    phi_o[...] = jnp.transpose(high).astype(BF16)
    plo_o[...] = jnp.transpose(low).astype(BF16)

    for cp in first:
        cp.wait_recv()
    total = part1[pl.ds(pl.multiple_of(r * share, 8), share)]
    for d in range(1, R):
        total += in1[d - 1]
    sketch_o[...] = total[:, :cols_dev]
    gtrail_o[...] = total[:, cols_dev:]
    e3 = (prow[:1, :] - c * cols_dev == lax.broadcasted_iota(jnp.int32, (cols_dev, panel), 0)).astype(F32)
    gpbuf[0] = full_dot(total[:, :cols_dev], e3)
    third = []
    for d in range(1, C):
        cp = pltpu.make_async_remote_copy(
            gpbuf.at[0], gpbuf.at[d], p_send.at[d - 1], p_recv.at[d - 1],
            device_id=(r, lax.rem(c + d, C)), device_id_type=MESH)
        cp.start()
        third.append(cp)

    for cp in second:
        cp.wait_recv()
    mine = pl.ds(pl.multiple_of(r * psh, 8), psh)
    total2 = part2[mine]
    for d in range(1, R):
        total2 += in2[d - 1]
    full[mine] = total2
    fourth = []
    for d in range(1, R):
        cp = pltpu.make_async_remote_copy(
            full.at[mine], full.at[mine], a_send.at[d - 1], a_recv.at[d - 1],
            device_id=(lax.rem(r + d, R), c), device_id_type=MESH)
        cp.start()
        fourth.append(cp)

    for cp in third:
        cp.wait_recv()
    gp = gpbuf[0]
    for d in range(1, C):
        gp += gpbuf[d]
    gpan_o[...] = gp
    for cp in fourth:
        cp.wait_recv()
    sums_o[...] = full[...]
    for cp in list(across.values()) + waits + relays + first + second + third + fourth:
        cp.wait_send()


def ordered(place, values):
    high = values.astype(BF16)
    rest = values - high.astype(F32)
    mid = rest.astype(BF16)
    low = (rest - mid.astype(F32)).astype(BF16)
    return (dot(place, low) + dot(place, mid)) + dot(place, high)


def gather_by_halves(R, C, mat, gau_in, piv, trl_in, sketch_o, gtrail_o, gpan_o, sums_o, phi_o, plo_o, place_o,
                     gau, trl, hbuf, lbuf, inx, pairs, gath, part1, near, far, in1, in_near, in_far, full_near, full_far, diag, gpbuf,
                     l_sem, x_send, x_recv, g_send, g_recv, y_send, y_recv, f_send, f_recv, s_send, s_recv, n_send, n_recv,
                     o_send, o_recv, an_send, an_recv, ao_send, ao_recv, p_send, p_recv, d_send, d_recv):
    r, c = lax.axis_index("rows"), lax.axis_index("cols")
    cols_dev, panel = mat.shape[1], piv.shape[1]
    depth = mat.shape[0]
    share = gau.shape[0] // R
    half = panel // 2
    hsh = half // R
    y, k = c // 2, c % 2
    partner = c + 1 - 2 * k
    opposite = lax.rem(c + 2, C)

    loads = [pltpu.make_async_copy(trl_in, trl, l_sem.at[0]), pltpu.make_async_copy(gau_in, gau, l_sem.at[1])]
    for cp in loads:
        cp.start()
    barrier = pltpu.get_barrier_semaphore()
    for d in range(1, C):
        pl.semaphore_signal(barrier, inc=1, device_id=(r, lax.rem(c + d, C)), device_id_type=MESH)
    for d in range(1, R):
        pl.semaphore_signal(barrier, inc=1, device_id=(lax.rem(r + d, R), c), device_id_type=MESH)

    prow = jnp.broadcast_to(piv[...], (panel, panel))
    pcol = jnp.transpose(prow.astype(F32)).astype(jnp.int32)
    brow = jnp.zeros_like(prow)
    bcol = jnp.zeros_like(prow)
    for b in range(1, C):
        brow += (prow >= b * cols_dev).astype(jnp.int32)
        bcol += (pcol >= b * cols_dev).astype(jnp.int32)
    sub = lax.broadcasted_iota(jnp.int32, (panel, panel), 0)
    lane = lax.broadcasted_iota(jnp.int32, (panel, panel), 1)
    same = brow == bcol
    rank_row = jnp.sum(jnp.where(same & (sub < lane), 1.0, 0.0), axis=0, keepdims=True)
    rank_col = jnp.sum(jnp.where(same & (lane < sub), 1.0, 0.0), axis=1, keepdims=True)
    slot_row = brow[:1, :] * MOST + rank_row.astype(jnp.int32)
    slot_col = bcol[:, :1] * MOST + rank_col.astype(jnp.int32)
    e1 = (slot_row - c * MOST == lax.broadcasted_iota(jnp.int32, (MOST, panel), 0)).astype(F32).astype(BF16)
    e2 = (pcol[:, :1] - c * cols_dev == lax.broadcasted_iota(jnp.int32, (panel, cols_dev), 1)).astype(F32).astype(BF16)
    sel = dot(e1, e2).astype(BF16)
    m2 = split(mat[...])
    gath[c] = dot(sel, m2[0], NT) + dot(sel, m2[1], NT)

    pl.semaphore_wait(barrier, C - 1 + R - 1)

    def block_copy(source, q, target, send, recv):
        piece = gath.at[source, pl.ds(q * (MOST // PARTS), MOST // PARTS)]
        return pltpu.make_async_remote_copy(piece, piece, send, recv, device_id=(r, target), device_id_type=MESH)

    def scatter(part, into, rows, send, recv):
        out = []
        for d in range(1, R):
            p = lax.rem(r + d, R)
            cp = pltpu.make_async_remote_copy(
                part.at[pl.ds(pl.multiple_of(p * rows, 8), rows)], into.at[d - 1], send.at[d - 1], recv.at[d - 1],
                device_id=(p, c), device_id_type=MESH)
            cp.start()
            out.append(cp)
        return out

    def finish(copies, part, into, rows):
        for cp in copies:
            cp.wait_recv()
        total = part[pl.ds(pl.multiple_of(r * rows, 8), rows)]
        for d in range(1, R):
            total += into[d - 1]
        return total

    def spread(total, whole, rows, send, recv):
        mine = pl.ds(pl.multiple_of(r * rows, 8), rows)
        whole[mine] = total
        out = []
        for d in range(1, R):
            cp = pltpu.make_async_remote_copy(
                whole.at[mine], whole.at[mine], send.at[d - 1], recv.at[d - 1],
                device_id=(lax.rem(r + d, R), c), device_id_type=MESH)
            cp.start()
            out.append(cp)
        return out

    across = [block_copy(c, q, opposite, y_send.at[q], y_recv.at[q]) for q in range(PARTS)]
    beside = [block_copy(c, q, partner, g_send.at[q], g_recv.at[q]) for q in range(PARTS)]
    relays = [block_copy(opposite, q, partner, f_send.at[q], f_recv.at[q]) for q in range(PARTS)]
    for cp in across + beside:
        cp.start()

    loads[0].wait()
    t2 = split(trl[...])
    for cp in beside:
        cp.wait_recv()
    own = gath[pl.ds(2 * y, 2)].reshape(half, depth)
    o2 = split(own)
    near[:, :half] = dot3(o2, o2, NT)
    near[:, half:] = dot3(o2, t2)
    near_out = scatter(near, in_near, hsh, n_send, n_recv)

    loads[1].wait()
    g2 = split(gau[...])
    part1[:, :cols_dev] = dot3(g2, m2)
    part1[:, cols_dev:] = dot3(g2, t2)
    side = lax.rem(r, 2)
    pair_out = []
    for i in range(R // 2):
        cp = pltpu.make_async_remote_copy(
            part1.at[pl.ds(pl.multiple_of((2 * i + 1 - side) * share, 8), share)], inx.at[i], x_send.at[i], x_recv.at[i],
            device_id=(r + 1 - 2 * side, c), device_id_type=MESH)
        cp.start()
        pair_out.append(cp)

    near_all = spread(finish(near_out, near, in_near, hsh), full_near, hsh, an_send, an_recv)
    across[0].wait_recv()
    relays[0].start()
    for cp in pair_out:
        cp.wait_recv()
    for i in range(R // 2):
        pairs[i] = part1[pl.ds(pl.multiple_of((2 * i + side) * share, 8), share)] + inx[i]
    sketch_out = []
    for d in range(1, R // 2):
        to = lax.rem(r // 2 + d, R // 2)
        cp = pltpu.make_async_remote_copy(
            pairs.at[to], in1.at[d - 1], s_send.at[d - 1], s_recv.at[d - 1],
            device_id=(2 * to + side, c), device_id_type=MESH)
        cp.start()
        sketch_out.append(cp)
    for q in range(1, PARTS):
        across[q].wait_recv()
        relays[q].start()
    own_t = jnp.transpose(own)
    t_high, t_low = split(own_t)
    hbuf[:, :half] = t_high
    lbuf[:, :half] = t_low
    for cp in near_all:
        cp.wait_recv()
    swap = pltpu.make_async_remote_copy(
        full_near.at[:, pl.ds(0, half)], diag, d_send.at[0], d_recv.at[0],
        device_id=(r, opposite), device_id_type=MESH)
    swap.start()
    for cp in relays:
        cp.wait_recv()

    other = gath[pl.ds(2 * (1 - y), 2)].reshape(half, depth)
    r2 = split(other)
    far[:, :half] = dot3(r2, o2, NT)
    far[:, half:] = dot3(r2, t2)
    far_out = scatter(far, in_far, hsh, o_send, o_recv)

    r_high, r_low = split(jnp.transpose(other))
    hbuf[:, half:] = r_high
    lbuf[:, half:] = r_low
    stores = [pltpu.make_async_copy(hbuf, phi_o, l_sem.at[2]), pltpu.make_async_copy(lbuf, plo_o, l_sem.at[3])]
    for cp in stores:
        cp.start()
    slot = lane + half * y
    slot = jnp.where(slot >= panel, slot - panel, slot)
    place = (slot_col == slot).astype(F32).astype(BF16)
    place_o[...] = place

    far_all = spread(finish(far_out, far, in_far, hsh), full_far, hsh, ao_send, ao_recv)

    for cp in sketch_out:
        cp.wait_recv()
    total = pairs[r // 2]
    for d in range(1, R // 2):
        total += in1[d - 1]
    sketch_o[...] = total[:, :cols_dev]
    gtrail_o[...] = total[:, cols_dev:]
    e3 = (prow[:1, :] - c * cols_dev == lax.broadcasted_iota(jnp.int32, (cols_dev, panel), 0)).astype(F32)
    gpbuf[0] = full_dot(total[:, :cols_dev], e3)
    third = []
    for d in range(1, C):
        cp = pltpu.make_async_remote_copy(
            gpbuf.at[0], gpbuf.at[d], p_send.at[d - 1], p_recv.at[d - 1],
            device_id=(r, lax.rem(c + d, C)), device_id_type=MESH)
        cp.start()
        third.append(cp)
    swap.wait_recv()
    for cp in far_all:
        cp.wait_recv()
    mixed = full_far[:, :half]
    first_rows = jnp.concatenate([full_near[:, :half], jnp.transpose(mixed), full_near[:, half:]], axis=1)
    last_rows = jnp.concatenate([mixed, diag[...], full_far[:, half:]], axis=1)
    by_rows = ordered(place, jnp.concatenate([first_rows, last_rows], axis=0))
    sums_o[:, panel:] = by_rows[:, panel:]
    sums_o[:, :panel] = ordered(place, jnp.transpose(by_rows[:, :panel]))
    for cp in third:
        cp.wait_recv()
    gp = gpbuf[0]
    for d in range(1, C):
        gp += gpbuf[d]
    gpan_o[...] = gp
    for cp in across + beside + relays + near_out + pair_out + sketch_out + near_all + far_out + far_all + third + [swap]:
        cp.wait_send()
    for cp in stores:
        cp.wait()


def factor_inverse(a):
    n = a.shape[0]
    rows = lax.broadcasted_iota(jnp.int32, (8, n), 0)
    lanes = lax.broadcasted_iota(jnp.int32, (8, n), 1)
    left = [a[8 * b:8 * b + 8, :] for b in range(n // 8)]
    right = [jnp.where(lanes == rows + 8 * b, 1.0, 0.0) for b in range(n // 8)]
    out = []
    for b0 in range(n // 8):
        x, y = left[b0], right[b0]
        cols = [jnp.broadcast_to(x[:, 8 * b0 + i:8 * b0 + i + 1], (8, n)) for i in range(8)]
        done = []
        for s in range(0, 8, 2):
            c0, c1 = cols[s], cols[s + 1]
            p, q, t = c0[s:s + 1], c0[s + 1:s + 2], c1[s + 1:s + 2]
            det = p * t - q * q
            inv = 1.0 / det
            ip, iq, it = t * inv, -q * inv, p * inv
            y0, y1 = y[s:s + 1], y[s + 1:s + 2]
            done.append(y0 * lax.rsqrt(p))
            done.append((y1 - (q / p) * y0) * lax.rsqrt(det / p))

            def eliminate(block):
                r0, r1 = block[s:s + 1], block[s + 1:s + 2]
                u0, u1 = ip * r0 + iq * r1, iq * r0 + it * r1
                return jnp.where(rows == s, u0, jnp.where(rows == s + 1, u1, block - c0 * u0 - c1 * u1))

            for i in range(s + 2, 8):
                cols[i] = eliminate(cols[i])
            x, y = eliminate(x), eliminate(y)
        out.append(jnp.concatenate(done, axis=0))
        for b in range(b0 + 1, n // 8):
            across = [jnp.broadcast_to(left[b][:, 8 * b0 + i:8 * b0 + i + 1], (8, n)) for i in range(8)]
            for i in range(8):
                left[b] = left[b] - across[i] * x[i:i + 1]
                right[b] = right[b] - across[i] * y[i:i + 1]
    return jnp.concatenate(out, axis=0)


def solve_and_project(sums, gtrail, gpan, place, sketch, phi, plo, trl, sketch_o, coupling_o, projected_o, tsk_o, hbuf, lbuf, tbuf, sems):
    copies = [pltpu.make_async_copy(a, b, sems.at[i])
              for i, (a, b) in enumerate(((phi, hbuf), (plo, lbuf), (trl, tbuf)))]
    for cp in copies:
        cp.start()
    sketch_o[...] = sketch[...]
    n = sums.shape[0]
    h = n // 2
    c1, c2 = sums[:h, n:], sums[h:, n:]
    i1 = factor_inverse(sums[:h, :h])
    l21 = full_dot(sums[h:, :h], i1, NT)
    k1 = full_dot(i1, c1)
    i2 = factor_inverse(sums[h:, h:n] - full_dot(l21, l21, NT))
    k2 = full_dot(i2, c2 - full_dot(l21, k1))
    coupling_o[:h, :] = k1
    coupling_o[h:, :] = k2
    w2 = full_dot(jnp.transpose(i2), k2)
    w1 = full_dot(jnp.transpose(i1), k1 - full_dot(jnp.transpose(l21), w2))
    weights = jnp.concatenate([w1, w2], axis=0)
    tsk_o[...] = gtrail[...] - full_dot(gpan[...], weights)
    w = tuple(dot(place[...], piece, TN).astype(BF16) for piece in split(weights))
    for cp in copies:
        cp.wait()
    projected_o[...] = tbuf[...] - dot3((hbuf[...], lbuf[...]), w)


def shards(R, C, matrix, gaussian, pivots, trailing):
    depth, cols_dev = matrix.shape
    sketch_rows = gaussian.shape[0]
    panel = pivots.shape[0]
    slab = trailing.shape[1]
    share, psh = sketch_rows // R, panel // R
    ny = max(C // 2 - 1, 1)
    vm = pl.BlockSpec(memory_space=pltpu.VMEM)
    anywhere = pl.BlockSpec(memory_space=pl.ANY)
    dma = pltpu.SemaphoreType.DMA
    if C == 4 and R % 2 == 0 and C * MOST == panel and panel == 2 * slab and (panel // 2) % (8 * R) == 0:
        half = panel // 2
        sketch, gtrail, gpan, sums, phi, plo, place = pl.pallas_call(
            functools.partial(gather_by_halves, R, C),
            out_shape=[
                jax.ShapeDtypeStruct((share, cols_dev), F32),
                jax.ShapeDtypeStruct((share, slab), F32),
                jax.ShapeDtypeStruct((share, panel), F32),
                jax.ShapeDtypeStruct((panel, panel + slab), F32),
                jax.ShapeDtypeStruct((depth, panel), BF16),
                jax.ShapeDtypeStruct((depth, panel), BF16),
                jax.ShapeDtypeStruct((panel, panel), BF16),
            ],
            in_specs=[vm, anywhere, vm, anywhere],
            out_specs=[vm] * 4 + [anywhere] * 2 + [vm],
            scratch_shapes=[
                pltpu.VMEM((sketch_rows, depth), F32),
                pltpu.VMEM((depth, slab), F32),
                pltpu.VMEM((depth, panel), BF16),
                pltpu.VMEM((depth, panel), BF16),
                pltpu.VMEM((R // 2, share, cols_dev + slab), F32),
                pltpu.VMEM((R // 2, share, cols_dev + slab), F32),
                pltpu.VMEM((C, MOST, depth), F32),
                pltpu.VMEM((sketch_rows, cols_dev + slab), F32),
                pltpu.VMEM((half, half + slab), F32),
                pltpu.VMEM((half, half + slab), F32),
                pltpu.VMEM((R - 1, share, cols_dev + slab), F32),
                pltpu.VMEM((R - 1, half // R, half + slab), F32),
                pltpu.VMEM((R - 1, half // R, half + slab), F32),
                pltpu.VMEM((half, half + slab), F32),
                pltpu.VMEM((half, half + slab), F32),
                pltpu.VMEM((half, half), F32),
                pltpu.VMEM((C, share, panel), F32),
                dma((4,)),
                *[dma((R // 2,))] * 2,
                *[dma((PARTS,))] * 6,
                *[dma((R - 1,))] * 10,
                *[dma((C - 1,))] * 2,
                *[dma((1,))] * 2,
            ],
            compiler_params=pltpu.CompilerParams(
                collective_id=0, has_side_effects=True, vmem_limit_bytes=56 * 1024 * 1024),
        )(matrix, gaussian, pivots.reshape(1, panel), trailing)
    else:
        sketch, gtrail, gpan, sums, phi, plo = pl.pallas_call(
            functools.partial(gather_and_sum, R, C),
            out_shape=[
                jax.ShapeDtypeStruct((share, cols_dev), F32),
                jax.ShapeDtypeStruct((share, slab), F32),
                jax.ShapeDtypeStruct((share, panel), F32),
                jax.ShapeDtypeStruct((panel, panel + slab), F32),
                jax.ShapeDtypeStruct((depth, panel), BF16),
                jax.ShapeDtypeStruct((depth, panel), BF16),
            ],
            in_specs=[vm] * 4,
            out_specs=[vm] * 6,
            scratch_shapes=[
                pltpu.VMEM((C, MOST, depth), F32),
                pltpu.VMEM((sketch_rows, cols_dev + slab), F32),
                pltpu.VMEM((panel, panel + slab), F32),
                pltpu.VMEM((R - 1, share, cols_dev + slab), F32),
                pltpu.VMEM((R - 1, psh, panel + slab), F32),
                pltpu.VMEM((panel, panel + slab), F32),
                pltpu.VMEM((C, share, panel), F32),
                dma((PARTS,)), dma((PARTS,)),
                dma((ny, PARTS)), dma((ny, PARTS)),
                dma((ny, PARTS)), dma((ny, PARTS)),
                dma((R - 1,)), dma((R - 1,)),
                dma((R - 1,)), dma((R - 1,)),
                dma((R - 1,)), dma((R - 1,)),
                dma((C - 1,)), dma((C - 1,)),
            ],
            compiler_params=pltpu.CompilerParams(
                collective_id=0, has_side_effects=True, vmem_limit_bytes=56 * 1024 * 1024),
        )(matrix, gaussian, pivots.reshape(1, panel), trailing)
        place = jnp.eye(panel, dtype=BF16)
    return pl.pallas_call(
        solve_and_project,
        out_shape=[
            jax.ShapeDtypeStruct((share, cols_dev), F32),
            jax.ShapeDtypeStruct((panel, slab), F32),
            jax.ShapeDtypeStruct((depth, slab), F32),
            jax.ShapeDtypeStruct((share, slab), F32),
        ],
        in_specs=[vm] * 5 + [anywhere] * 3,
        out_specs=[vm] * 4,
        scratch_shapes=[
            pltpu.VMEM((depth, panel), BF16),
            pltpu.VMEM((depth, panel), BF16),
            pltpu.VMEM((depth, slab), F32),
            dma((3,)),
        ],
        compiler_params=pltpu.CompilerParams(vmem_limit_bytes=56 * 1024 * 1024),
    )(sums, gtrail, gpan, place, sketch, phi, plo, trailing)


def solution(mesh):
    placed = (P("rows", "cols"), P(None, "rows"), P(), P("rows", "cols"))
    return jax.shard_map(
        functools.partial(shards, mesh.shape["rows"], mesh.shape["cols"]),
        mesh=mesh,
        in_specs=placed,
        out_specs=(P("rows", "cols"), P(None, "cols"), P("rows", "cols"), P("rows", "cols")),
        check_vma=False,
    )
```

```python
import functools

import jax
import jax.numpy as jnp
from jax import lax
from jax.experimental import pallas as pl
from jax.experimental.pallas import tpu as pltpu
from jax.sharding import PartitionSpec as P

MESH = pl.DeviceIdType.MESH
MOST = 64
PARTS = 4
F32 = jnp.float32
BF16 = jnp.bfloat16
NN = (((1,), (0,)), ((), ()))
NT = (((1,), (1,)), ((), ()))
TN = (((0,), (0,)), ((), ()))


def split(values):
    high = values.astype(BF16)
    return high, (values - high.astype(F32)).astype(BF16)


def dot(left, right, dims=NN):
    return lax.dot_general(left, right, dims, preferred_element_type=F32)


def dot3(left, right, dims=NN):
    return dot(left[0], right[0], dims) + (dot(left[0], right[1], dims) + dot(left[1], right[0], dims))


def full_dot(left, right, dims=NN):
    return lax.dot_general(left, right, dims, precision=lax.Precision.HIGHEST, preferred_element_type=F32)


def gather_and_sum(R, C, mat, gau, piv, trl, sketch_o, gtrail_o, gpan_o, sums_o, phi_o, plo_o,
                   gath, part1, part2, in1, in2, full, gpbuf,
                   g_send, g_recv, y_send, y_recv, f_send, f_recv, s1_send, s1_recv, s2_send, s2_recv,
                   a_send, a_recv, p_send, p_recv):
    r, c = lax.axis_index("rows"), lax.axis_index("cols")
    cols_dev, panel = mat.shape[1], piv.shape[1]
    share = gau.shape[0] // R
    psh = panel // R
    ny = C // 2
    y, k = c // 2, c % 2
    partner = c + 1 - 2 * k

    barrier = pltpu.get_barrier_semaphore()
    for d in range(1, C):
        pl.semaphore_signal(barrier, inc=1, device_id=(r, lax.rem(c + d, C)), device_id_type=MESH)
    for d in range(1, R):
        pl.semaphore_signal(barrier, inc=1, device_id=(lax.rem(r + d, R), c), device_id_type=MESH)

    prow = jnp.broadcast_to(piv[...], (panel, panel))
    pcol = jnp.transpose(prow.astype(F32)).astype(jnp.int32)
    brow = jnp.zeros_like(prow)
    bcol = jnp.zeros_like(prow)
    for b in range(1, C):
        brow += (prow >= b * cols_dev).astype(jnp.int32)
        bcol += (pcol >= b * cols_dev).astype(jnp.int32)
    sub = lax.broadcasted_iota(jnp.int32, (panel, panel), 0)
    lane = lax.broadcasted_iota(jnp.int32, (panel, panel), 1)
    same = brow == bcol
    rank_row = jnp.sum(jnp.where(same & (sub < lane), 1.0, 0.0), axis=0, keepdims=True)
    rank_col = jnp.sum(jnp.where(same & (lane < sub), 1.0, 0.0), axis=1, keepdims=True)
    slot_row = brow[:1, :] * MOST + rank_row.astype(jnp.int32)
    slot_col = bcol[:, :1] * MOST + rank_col.astype(jnp.int32)
    e1 = (slot_row - c * MOST == lax.broadcasted_iota(jnp.int32, (MOST, panel), 0)).astype(F32).astype(BF16)
    e2 = (pcol[:, :1] - c * cols_dev == lax.broadcasted_iota(jnp.int32, (panel, cols_dev), 1)).astype(F32).astype(BF16)
    sel = dot(e1, e2).astype(BF16)
    m2 = split(mat[...])
    gath[c] = dot(sel, m2[0], NT) + dot(sel, m2[1], NT)

    pl.semaphore_wait(barrier, C - 1 + R - 1)

    def block_copy(source, q, target, send, recv):
        piece = gath.at[source, pl.ds(q * (MOST // PARTS), MOST // PARTS)]
        return pltpu.make_async_remote_copy(piece, piece, send, recv, device_id=(r, target), device_id_type=MESH)

    waits = []
    across = {}
    for q in range(PARTS):
        for d in range(1, ny):
            cp = block_copy(c, q, lax.rem(y + d, ny) * 2 + k, y_send.at[d - 1, q], y_recv.at[d - 1, q])
            cp.start()
            across[d, q] = cp
    for q in range(PARTS):
        cp = block_copy(c, q, partner, g_send.at[q], g_recv.at[q])
        cp.start()
        waits.append(cp)

    g2 = split(gau[...])
    t2 = split(trl[...])
    part1[:, :cols_dev] = dot3(g2, m2)
    part1[:, cols_dev:] = dot3(g2, t2)

    def scatter(part, into, rows, send, recv):
        out = []
        for d in range(1, R):
            p = lax.rem(r + d, R)
            cp = pltpu.make_async_remote_copy(
                part.at[pl.ds(pl.multiple_of(p * rows, 8), rows)], into.at[d - 1], send.at[d - 1], recv.at[d - 1],
                device_id=(p, c), device_id_type=MESH)
            cp.start()
            out.append(cp)
        return out

    first = scatter(part1, in1, share, s1_send, s1_recv)

    relays = []
    for q in range(PARTS):
        for d in range(1, ny):
            across[d, q].wait_recv()
            source = lax.rem(y + ny - d, ny) * 2 + k
            cp = block_copy(source, q, partner, f_send.at[d - 1, q], f_recv.at[d - 1, q])
            cp.start()
            relays.append(cp)
    for cp in waits:
        cp.wait_recv()
    for cp in relays:
        cp.wait_recv()

    place = (slot_col == lax.broadcasted_iota(jnp.int32, (panel, C * MOST), 1)).astype(F32).astype(BF16)
    got = split(gath[...].reshape(C * MOST, gath.shape[2]))
    high = dot(place, got[0])
    low = dot(place, got[1])
    p2 = (high.astype(BF16), low.astype(BF16))
    hl = dot(p2[0], p2[1], NT)
    part2[:, :panel] = dot(p2[0], p2[0], NT) + (hl + jnp.transpose(hl))
    part2[:, panel:] = dot3(p2, t2)
    second = scatter(part2, in2, psh, s2_send, s2_recv)

    phi_o[...] = jnp.transpose(high).astype(BF16)
    plo_o[...] = jnp.transpose(low).astype(BF16)

    for cp in first:
        cp.wait_recv()
    total = part1[pl.ds(pl.multiple_of(r * share, 8), share)]
    for d in range(1, R):
        total += in1[d - 1]
    sketch_o[...] = total[:, :cols_dev]
    gtrail_o[...] = total[:, cols_dev:]
    e3 = (prow[:1, :] - c * cols_dev == lax.broadcasted_iota(jnp.int32, (cols_dev, panel), 0)).astype(F32)
    gpbuf[0] = full_dot(total[:, :cols_dev], e3)
    third = []
    for d in range(1, C):
        cp = pltpu.make_async_remote_copy(
            gpbuf.at[0], gpbuf.at[d], p_send.at[d - 1], p_recv.at[d - 1],
            device_id=(r, lax.rem(c + d, C)), device_id_type=MESH)
        cp.start()
        third.append(cp)

    for cp in second:
        cp.wait_recv()
    mine = pl.ds(pl.multiple_of(r * psh, 8), psh)
    total2 = part2[mine]
    for d in range(1, R):
        total2 += in2[d - 1]
    full[mine] = total2
    fourth = []
    for d in range(1, R):
        cp = pltpu.make_async_remote_copy(
            full.at[mine], full.at[mine], a_send.at[d - 1], a_recv.at[d - 1],
            device_id=(lax.rem(r + d, R), c), device_id_type=MESH)
        cp.start()
        fourth.append(cp)

    for cp in third:
        cp.wait_recv()
    gp = gpbuf[0]
    for d in range(1, C):
        gp += gpbuf[d]
    gpan_o[...] = gp
    for cp in fourth:
        cp.wait_recv()
    sums_o[...] = full[...]
    for cp in list(across.values()) + waits + relays + first + second + third + fourth:
        cp.wait_send()


def ordered(place, values):
    high = values.astype(BF16)
    rest = values - high.astype(F32)
    mid = rest.astype(BF16)
    low = (rest - mid.astype(F32)).astype(BF16)
    return (dot(place, low) + dot(place, mid)) + dot(place, high)


def gather_by_halves(R, C, mat, gau_in, piv, trl_in, sketch_o, gtrail_o, gpan_o, sums_o, phi_o, plo_o, place_o,
                     gau, trl, hbuf, lbuf, inx, pairs, gath, part1, near, far, in1, in_near, in_far, full_near, full_far, diag, gpbuf,
                     l_sem, x_send, x_recv, g_send, g_recv, y_send, y_recv, f_send, f_recv, s_send, s_recv, n_send, n_recv,
                     o_send, o_recv, an_send, an_recv, ao_send, ao_recv, p_send, p_recv, d_send, d_recv):
    r, c = lax.axis_index("rows"), lax.axis_index("cols")
    cols_dev, panel = mat.shape[1], piv.shape[1]
    depth = mat.shape[0]
    share = gau.shape[0] // R
    half = panel // 2
    hsh = half // R
    y, k = c // 2, c % 2
    partner = c + 1 - 2 * k
    opposite = lax.rem(c + 2, C)

    loads = [pltpu.make_async_copy(trl_in, trl, l_sem.at[0]), pltpu.make_async_copy(gau_in, gau, l_sem.at[1])]
    for cp in loads:
        cp.start()
    barrier = pltpu.get_barrier_semaphore()
    for d in range(1, C):
        pl.semaphore_signal(barrier, inc=1, device_id=(r, lax.rem(c + d, C)), device_id_type=MESH)
    for d in range(1, R):
        pl.semaphore_signal(barrier, inc=1, device_id=(lax.rem(r + d, R), c), device_id_type=MESH)

    prow = jnp.broadcast_to(piv[...], (panel, panel))
    pcol = jnp.transpose(prow.astype(F32)).astype(jnp.int32)
    brow = jnp.zeros_like(prow)
    bcol = jnp.zeros_like(prow)
    for b in range(1, C):
        brow += (prow >= b * cols_dev).astype(jnp.int32)
        bcol += (pcol >= b * cols_dev).astype(jnp.int32)
    sub = lax.broadcasted_iota(jnp.int32, (panel, panel), 0)
    lane = lax.broadcasted_iota(jnp.int32, (panel, panel), 1)
    same = brow == bcol
    rank_row = jnp.sum(jnp.where(same & (sub < lane), 1.0, 0.0), axis=0, keepdims=True)
    rank_col = jnp.sum(jnp.where(same & (lane < sub), 1.0, 0.0), axis=1, keepdims=True)
    slot_row = brow[:1, :] * MOST + rank_row.astype(jnp.int32)
    slot_col = bcol[:, :1] * MOST + rank_col.astype(jnp.int32)
    e1 = (slot_row - c * MOST == lax.broadcasted_iota(jnp.int32, (MOST, panel), 0)).astype(F32).astype(BF16)
    e2 = (pcol[:, :1] - c * cols_dev == lax.broadcasted_iota(jnp.int32, (panel, cols_dev), 1)).astype(F32).astype(BF16)
    sel = dot(e1, e2).astype(BF16)
    m2 = split(mat[...])
    gath[c] = dot(sel, m2[0], NT) + dot(sel, m2[1], NT)

    pl.semaphore_wait(barrier, C - 1 + R - 1)

    def block_copy(source, q, target, send, recv):
        piece = gath.at[source, pl.ds(q * (MOST // PARTS), MOST // PARTS)]
        return pltpu.make_async_remote_copy(piece, piece, send, recv, device_id=(r, target), device_id_type=MESH)

    def scatter(part, into, rows, send, recv):
        out = []
        for d in range(1, R):
            p = lax.rem(r + d, R)
            cp = pltpu.make_async_remote_copy(
                part.at[pl.ds(pl.multiple_of(p * rows, 8), rows)], into.at[d - 1], send.at[d - 1], recv.at[d - 1],
                device_id=(p, c), device_id_type=MESH)
            cp.start()
            out.append(cp)
        return out

    def finish(copies, part, into, rows):
        for cp in copies:
            cp.wait_recv()
        total = part[pl.ds(pl.multiple_of(r * rows, 8), rows)]
        for d in range(1, R):
            total += into[d - 1]
        return total

    def spread(total, whole, rows, send, recv):
        mine = pl.ds(pl.multiple_of(r * rows, 8), rows)
        whole[mine] = total
        out = []
        for d in range(1, R):
            cp = pltpu.make_async_remote_copy(
                whole.at[mine], whole.at[mine], send.at[d - 1], recv.at[d - 1],
                device_id=(lax.rem(r + d, R), c), device_id_type=MESH)
            cp.start()
            out.append(cp)
        return out

    across = [block_copy(c, q, opposite, y_send.at[q], y_recv.at[q]) for q in range(PARTS)]
    beside = [block_copy(c, q, partner, g_send.at[q], g_recv.at[q]) for q in range(PARTS)]
    relays = [block_copy(opposite, q, partner, f_send.at[q], f_recv.at[q]) for q in range(PARTS)]
    for cp in across + beside:
        cp.start()

    loads[0].wait()
    t2 = split(trl[...])
    for cp in beside:
        cp.wait_recv()
    own = gath[pl.ds(2 * y, 2)].reshape(half, depth)
    o2 = split(own)
    near[:, :half] = dot3(o2, o2, NT)
    near[:, half:] = dot3(o2, t2)
    near_out = scatter(near, in_near, hsh, n_send, n_recv)

    loads[1].wait()
    g2 = split(gau[...])
    part1[:, :cols_dev] = dot3(g2, m2)
    part1[:, cols_dev:] = dot3(g2, t2)
    side = lax.rem(r, 2)
    pair_out = []
    for i in range(R // 2):
        cp = pltpu.make_async_remote_copy(
            part1.at[pl.ds(pl.multiple_of((2 * i + 1 - side) * share, 8), share)], inx.at[i], x_send.at[i], x_recv.at[i],
            device_id=(r + 1 - 2 * side, c), device_id_type=MESH)
        cp.start()
        pair_out.append(cp)

    near_all = spread(finish(near_out, near, in_near, hsh), full_near, hsh, an_send, an_recv)
    across[0].wait_recv()
    relays[0].start()
    for cp in pair_out:
        cp.wait_recv()
    for i in range(R // 2):
        pairs[i] = part1[pl.ds(pl.multiple_of((2 * i + side) * share, 8), share)] + inx[i]
    sketch_out = []
    for d in range(1, R // 2):
        to = lax.rem(r // 2 + d, R // 2)
        cp = pltpu.make_async_remote_copy(
            pairs.at[to], in1.at[d - 1], s_send.at[d - 1], s_recv.at[d - 1],
            device_id=(2 * to + side, c), device_id_type=MESH)
        cp.start()
        sketch_out.append(cp)
    across[1].wait_recv()
    relays[1].start()

    group = MOST // 2

    def far_sums(h):
        for q in range(h * PARTS // 2, (h + 1) * PARTS // 2):
            relays[q].wait_recv()
        values = gath[pl.ds(2 * (1 - y), 2), h * group:(h + 1) * group].reshape(half // 2, depth)
        r2 = split(values)
        far[h, :, :half] = dot3(r2, o2, NT)
        far[h, :, half:] = dot3(r2, t2)
        return scatter(far.at[h], in_far.at[h], hsh // 2, o_send.at[h], o_recv.at[h])

    def far_spread(h):
        total = finish(far_out[h], far.at[h], in_far.at[h], hsh // 2)
        return spread(total, full_far.at[h], hsh // 2, ao_send.at[h], ao_recv.at[h])

    far_out = [far_sums(0)]
    across[2].wait_recv()
    relays[2].start()
    t_high, t_low = split(jnp.transpose(own))
    hbuf[:, :half] = t_high
    lbuf[:, :half] = t_low
    for cp in near_all:
        cp.wait_recv()
    swap = pltpu.make_async_remote_copy(
        full_near.at[:, pl.ds(0, half)], diag, d_send.at[0], d_recv.at[0],
        device_id=(r, opposite), device_id_type=MESH)
    for q in range(3, PARTS):
        across[q].wait_recv()
        relays[q].start()
    swap.start()
    far_all = far_spread(0)
    far_out.append(far_sums(1))

    other = gath[pl.ds(2 * (1 - y), 2)].reshape(half, depth)
    r_high, r_low = split(jnp.transpose(other))
    hbuf[:, half:] = r_high
    lbuf[:, half:] = r_low
    stores = [pltpu.make_async_copy(hbuf, phi_o, l_sem.at[2]), pltpu.make_async_copy(lbuf, plo_o, l_sem.at[3])]
    for cp in stores:
        cp.start()
    slot = lane + half * y
    slot = jnp.where(slot >= panel, slot - panel, slot)
    place = (slot_col == slot).astype(F32).astype(BF16)
    place_o[...] = place

    far_all = far_all + far_spread(1)

    for cp in sketch_out:
        cp.wait_recv()
    total = pairs[r // 2]
    for d in range(1, R // 2):
        total += in1[d - 1]
    sketch_o[...] = total[:, :cols_dev]
    gtrail_o[...] = total[:, cols_dev:]
    e3 = (prow[:1, :] - c * cols_dev == lax.broadcasted_iota(jnp.int32, (cols_dev, panel), 0)).astype(F32)
    gpbuf[0] = full_dot(total[:, :cols_dev], e3)
    third = []
    for d in range(1, C):
        cp = pltpu.make_async_remote_copy(
            gpbuf.at[0], gpbuf.at[d], p_send.at[d - 1], p_recv.at[d - 1],
            device_id=(r, lax.rem(c + d, C)), device_id_type=MESH)
        cp.start()
        third.append(cp)
    swap.wait_recv()
    for cp in far_all:
        cp.wait_recv()
    whole = jnp.concatenate(
        [full_far[h, i * group:(i + 1) * group] for i in range(2) for h in range(2)], axis=0)
    mixed = whole[:, :half]
    first_rows = jnp.concatenate([full_near[:, :half], jnp.transpose(mixed), full_near[:, half:]], axis=1)
    last_rows = jnp.concatenate([mixed, diag[...], whole[:, half:]], axis=1)
    by_rows = ordered(place, jnp.concatenate([first_rows, last_rows], axis=0))
    sums_o[:, panel:] = by_rows[:, panel:]
    sums_o[:, :panel] = ordered(place, jnp.transpose(by_rows[:, :panel]))
    for cp in third:
        cp.wait_recv()
    gp = gpbuf[0]
    for d in range(1, C):
        gp += gpbuf[d]
    gpan_o[...] = gp
    for cp in across + beside + relays + near_out + pair_out + sketch_out + near_all + far_out[0] + far_out[1] + far_all + third + [swap]:
        cp.wait_send()
    for cp in stores:
        cp.wait()


def factor_inverse(a):
    n = a.shape[0]
    rows = lax.broadcasted_iota(jnp.int32, (8, n), 0)
    lanes = lax.broadcasted_iota(jnp.int32, (8, n), 1)
    left = [a[8 * b:8 * b + 8, :] for b in range(n // 8)]
    right = [jnp.where(lanes == rows + 8 * b, 1.0, 0.0) for b in range(n // 8)]
    out = []
    for b0 in range(n // 8):
        x, y = left[b0], right[b0]
        cols = [jnp.broadcast_to(x[:, 8 * b0 + i:8 * b0 + i + 1], (8, n)) for i in range(8)]
        done = []
        for s in range(0, 8, 2):
            c0, c1 = cols[s], cols[s + 1]
            p, q, t = c0[s:s + 1], c0[s + 1:s + 2], c1[s + 1:s + 2]
            det = p * t - q * q
            inv = 1.0 / det
            ip, iq, it = t * inv, -q * inv, p * inv
            y0, y1 = y[s:s + 1], y[s + 1:s + 2]
            done.append(y0 * lax.rsqrt(p))
            done.append((y1 - (q / p) * y0) * lax.rsqrt(det / p))

            def eliminate(block):
                r0, r1 = block[s:s + 1], block[s + 1:s + 2]
                u0, u1 = ip * r0 + iq * r1, iq * r0 + it * r1
                return jnp.where(rows == s, u0, jnp.where(rows == s + 1, u1, block - c0 * u0 - c1 * u1))

            for i in range(s + 2, 8):
                cols[i] = eliminate(cols[i])
            x, y = eliminate(x), eliminate(y)
        out.append(jnp.concatenate(done, axis=0))
        for b in range(b0 + 1, n // 8):
            across = [jnp.broadcast_to(left[b][:, 8 * b0 + i:8 * b0 + i + 1], (8, n)) for i in range(8)]
            for i in range(8):
                left[b] = left[b] - across[i] * x[i:i + 1]
                right[b] = right[b] - across[i] * y[i:i + 1]
    return jnp.concatenate(out, axis=0)


def solve_and_project(sums, gtrail, gpan, place, sketch, phi, plo, trl, sketch_o, coupling_o, projected_o, tsk_o, hbuf, lbuf, tbuf, sems):
    copies = [pltpu.make_async_copy(a, b, sems.at[i])
              for i, (a, b) in enumerate(((phi, hbuf), (plo, lbuf), (trl, tbuf)))]
    for cp in copies:
        cp.start()
    sketch_o[...] = sketch[...]
    n = sums.shape[0]
    h = n // 2
    c1, c2 = sums[:h, n:], sums[h:, n:]
    i1 = factor_inverse(sums[:h, :h])
    l21 = full_dot(sums[h:, :h], i1, NT)
    k1 = full_dot(i1, c1)
    i2 = factor_inverse(sums[h:, h:n] - full_dot(l21, l21, NT))
    k2 = full_dot(i2, c2 - full_dot(l21, k1))
    coupling_o[:h, :] = k1
    coupling_o[h:, :] = k2
    w2 = full_dot(jnp.transpose(i2), k2)
    w1 = full_dot(jnp.transpose(i1), k1 - full_dot(jnp.transpose(l21), w2))
    weights = jnp.concatenate([w1, w2], axis=0)
    tsk_o[...] = gtrail[...] - full_dot(gpan[...], weights)
    w = tuple(dot(place[...], piece, TN).astype(BF16) for piece in split(weights))
    for cp in copies:
        cp.wait()
    projected_o[...] = tbuf[...] - dot3((hbuf[...], lbuf[...]), w)


def shards(R, C, matrix, gaussian, pivots, trailing):
    depth, cols_dev = matrix.shape
    sketch_rows = gaussian.shape[0]
    panel = pivots.shape[0]
    slab = trailing.shape[1]
    share, psh = sketch_rows // R, panel // R
    ny = max(C // 2 - 1, 1)
    vm = pl.BlockSpec(memory_space=pltpu.VMEM)
    anywhere = pl.BlockSpec(memory_space=pl.ANY)
    dma = pltpu.SemaphoreType.DMA
    if C == 4 and R % 2 == 0 and C * MOST == panel and panel == 2 * slab and panel % (32 * R) == 0:
        half = panel // 2
        sketch, gtrail, gpan, sums, phi, plo, place = pl.pallas_call(
            functools.partial(gather_by_halves, R, C),
            out_shape=[
                jax.ShapeDtypeStruct((share, cols_dev), F32),
                jax.ShapeDtypeStruct((share, slab), F32),
                jax.ShapeDtypeStruct((share, panel), F32),
                jax.ShapeDtypeStruct((panel, panel + slab), F32),
                jax.ShapeDtypeStruct((depth, panel), BF16),
                jax.ShapeDtypeStruct((depth, panel), BF16),
                jax.ShapeDtypeStruct((panel, panel), BF16),
            ],
            in_specs=[vm, anywhere, vm, anywhere],
            out_specs=[vm] * 4 + [anywhere] * 2 + [vm],
            scratch_shapes=[
                pltpu.VMEM((sketch_rows, depth), F32),
                pltpu.VMEM((depth, slab), F32),
                pltpu.VMEM((depth, panel), BF16),
                pltpu.VMEM((depth, panel), BF16),
                pltpu.VMEM((R // 2, share, cols_dev + slab), F32),
                pltpu.VMEM((R // 2, share, cols_dev + slab), F32),
                pltpu.VMEM((C, MOST, depth), F32),
                pltpu.VMEM((sketch_rows, cols_dev + slab), F32),
                pltpu.VMEM((half, half + slab), F32),
                pltpu.VMEM((2, half // 2, half + slab), F32),
                pltpu.VMEM((R - 1, share, cols_dev + slab), F32),
                pltpu.VMEM((R - 1, half // R, half + slab), F32),
                pltpu.VMEM((2, R - 1, half // (2 * R), half + slab), F32),
                pltpu.VMEM((half, half + slab), F32),
                pltpu.VMEM((2, half // 2, half + slab), F32),
                pltpu.VMEM((half, half), F32),
                pltpu.VMEM((C, share, panel), F32),
                dma((4,)),
                *[dma((R // 2,))] * 2,
                *[dma((PARTS,))] * 6,
                *[dma((R - 1,))] * 4,
                *[dma((2, R - 1))] * 2,
                *[dma((R - 1,))] * 2,
                *[dma((2, R - 1))] * 2,
                *[dma((C - 1,))] * 2,
                *[dma((1,))] * 2,
            ],
            compiler_params=pltpu.CompilerParams(
                collective_id=0, has_side_effects=True, vmem_limit_bytes=56 * 1024 * 1024),
        )(matrix, gaussian, pivots.reshape(1, panel), trailing)
    else:
        sketch, gtrail, gpan, sums, phi, plo = pl.pallas_call(
            functools.partial(gather_and_sum, R, C),
            out_shape=[
                jax.ShapeDtypeStruct((share, cols_dev), F32),
                jax.ShapeDtypeStruct((share, slab), F32),
                jax.ShapeDtypeStruct((share, panel), F32),
                jax.ShapeDtypeStruct((panel, panel + slab), F32),
                jax.ShapeDtypeStruct((depth, panel), BF16),
                jax.ShapeDtypeStruct((depth, panel), BF16),
            ],
            in_specs=[vm] * 4,
            out_specs=[vm] * 6,
            scratch_shapes=[
                pltpu.VMEM((C, MOST, depth), F32),
                pltpu.VMEM((sketch_rows, cols_dev + slab), F32),
                pltpu.VMEM((panel, panel + slab), F32),
                pltpu.VMEM((R - 1, share, cols_dev + slab), F32),
                pltpu.VMEM((R - 1, psh, panel + slab), F32),
                pltpu.VMEM((panel, panel + slab), F32),
                pltpu.VMEM((C, share, panel), F32),
                dma((PARTS,)), dma((PARTS,)),
                dma((ny, PARTS)), dma((ny, PARTS)),
                dma((ny, PARTS)), dma((ny, PARTS)),
                dma((R - 1,)), dma((R - 1,)),
                dma((R - 1,)), dma((R - 1,)),
                dma((R - 1,)), dma((R - 1,)),
                dma((C - 1,)), dma((C - 1,)),
            ],
            compiler_params=pltpu.CompilerParams(
                collective_id=0, has_side_effects=True, vmem_limit_bytes=56 * 1024 * 1024),
        )(matrix, gaussian, pivots.reshape(1, panel), trailing)
        place = jnp.eye(panel, dtype=BF16)
    return pl.pallas_call(
        solve_and_project,
        out_shape=[
            jax.ShapeDtypeStruct((share, cols_dev), F32),
            jax.ShapeDtypeStruct((panel, slab), F32),
            jax.ShapeDtypeStruct((depth, slab), F32),
            jax.ShapeDtypeStruct((share, slab), F32),
        ],
        in_specs=[vm] * 5 + [anywhere] * 3,
        out_specs=[vm] * 4,
        scratch_shapes=[
            pltpu.VMEM((depth, panel), BF16),
            pltpu.VMEM((depth, panel), BF16),
            pltpu.VMEM((depth, slab), F32),
            dma((3,)),
        ],
        compiler_params=pltpu.CompilerParams(vmem_limit_bytes=56 * 1024 * 1024),
    )(sums, gtrail, gpan, place, sketch, phi, plo, trailing)


def solution(mesh):
    placed = (P("rows", "cols"), P(None, "rows"), P(), P("rows", "cols"))
    return jax.shard_map(
        functools.partial(shards, mesh.shape["rows"], mesh.shape["cols"]),
        mesh=mesh,
        in_specs=placed,
        out_specs=(P("rows", "cols"), P(None, "cols"), P("rows", "cols"), P("rows", "cols")),
        check_vma=False,
    )
```

```python
import functools

import jax
import jax.numpy as jnp
from jax import lax
from jax.experimental import pallas as pl
from jax.experimental.pallas import tpu as pltpu
from jax.sharding import PartitionSpec as P

MESH = pl.DeviceIdType.MESH
MOST = 64
PARTS = 4
F32 = jnp.float32
BF16 = jnp.bfloat16
NN = (((1,), (0,)), ((), ()))
NT = (((1,), (1,)), ((), ()))
TN = (((0,), (0,)), ((), ()))


def split(values):
    high = values.astype(BF16)
    return high, (values - high.astype(F32)).astype(BF16)


def dot(left, right, dims=NN):
    return lax.dot_general(left, right, dims, preferred_element_type=F32)


def dot3(left, right, dims=NN):
    return dot(left[0], right[0], dims) + (dot(left[0], right[1], dims) + dot(left[1], right[0], dims))


def full_dot(left, right, dims=NN):
    return lax.dot_general(left, right, dims, precision=lax.Precision.HIGHEST, preferred_element_type=F32)


def gather_and_sum(R, C, mat, gau, piv, trl, sketch_o, gtrail_o, gpan_o, sums_o, phi_o, plo_o,
                   gath, part1, part2, in1, in2, full, gpbuf,
                   g_send, g_recv, y_send, y_recv, f_send, f_recv, s1_send, s1_recv, s2_send, s2_recv,
                   a_send, a_recv, p_send, p_recv):
    r, c = lax.axis_index("rows"), lax.axis_index("cols")
    cols_dev, panel = mat.shape[1], piv.shape[1]
    share = gau.shape[0] // R
    psh = panel // R
    ny = C // 2
    y, k = c // 2, c % 2
    partner = c + 1 - 2 * k

    barrier = pltpu.get_barrier_semaphore()
    for d in range(1, C):
        pl.semaphore_signal(barrier, inc=1, device_id=(r, lax.rem(c + d, C)), device_id_type=MESH)
    for d in range(1, R):
        pl.semaphore_signal(barrier, inc=1, device_id=(lax.rem(r + d, R), c), device_id_type=MESH)

    prow = jnp.broadcast_to(piv[...], (panel, panel))
    pcol = jnp.transpose(prow.astype(F32)).astype(jnp.int32)
    brow = jnp.zeros_like(prow)
    bcol = jnp.zeros_like(prow)
    for b in range(1, C):
        brow += (prow >= b * cols_dev).astype(jnp.int32)
        bcol += (pcol >= b * cols_dev).astype(jnp.int32)
    sub = lax.broadcasted_iota(jnp.int32, (panel, panel), 0)
    lane = lax.broadcasted_iota(jnp.int32, (panel, panel), 1)
    same = brow == bcol
    rank_row = jnp.sum(jnp.where(same & (sub < lane), 1.0, 0.0), axis=0, keepdims=True)
    rank_col = jnp.sum(jnp.where(same & (lane < sub), 1.0, 0.0), axis=1, keepdims=True)
    slot_row = brow[:1, :] * MOST + rank_row.astype(jnp.int32)
    slot_col = bcol[:, :1] * MOST + rank_col.astype(jnp.int32)
    e1 = (slot_row - c * MOST == lax.broadcasted_iota(jnp.int32, (MOST, panel), 0)).astype(F32).astype(BF16)
    e2 = (pcol[:, :1] - c * cols_dev == lax.broadcasted_iota(jnp.int32, (panel, cols_dev), 1)).astype(F32).astype(BF16)
    sel = dot(e1, e2).astype(BF16)
    m2 = split(mat[...])
    gath[c] = dot(sel, m2[0], NT) + dot(sel, m2[1], NT)

    pl.semaphore_wait(barrier, C - 1 + R - 1)

    def block_copy(source, q, target, send, recv):
        piece = gath.at[source, pl.ds(q * (MOST // PARTS), MOST // PARTS)]
        return pltpu.make_async_remote_copy(piece, piece, send, recv, device_id=(r, target), device_id_type=MESH)

    waits = []
    across = {}
    for q in range(PARTS):
        for d in range(1, ny):
            cp = block_copy(c, q, lax.rem(y + d, ny) * 2 + k, y_send.at[d - 1, q], y_recv.at[d - 1, q])
            cp.start()
            across[d, q] = cp
    for q in range(PARTS):
        cp = block_copy(c, q, partner, g_send.at[q], g_recv.at[q])
        cp.start()
        waits.append(cp)

    g2 = split(gau[...])
    t2 = split(trl[...])
    part1[:, :cols_dev] = dot3(g2, m2)
    part1[:, cols_dev:] = dot3(g2, t2)

    def scatter(part, into, rows, send, recv):
        out = []
        for d in range(1, R):
            p = lax.rem(r + d, R)
            cp = pltpu.make_async_remote_copy(
                part.at[pl.ds(pl.multiple_of(p * rows, 8), rows)], into.at[d - 1], send.at[d - 1], recv.at[d - 1],
                device_id=(p, c), device_id_type=MESH)
            cp.start()
            out.append(cp)
        return out

    first = scatter(part1, in1, share, s1_send, s1_recv)

    relays = []
    for q in range(PARTS):
        for d in range(1, ny):
            across[d, q].wait_recv()
            source = lax.rem(y + ny - d, ny) * 2 + k
            cp = block_copy(source, q, partner, f_send.at[d - 1, q], f_recv.at[d - 1, q])
            cp.start()
            relays.append(cp)
    for cp in waits:
        cp.wait_recv()
    for cp in relays:
        cp.wait_recv()

    place = (slot_col == lax.broadcasted_iota(jnp.int32, (panel, C * MOST), 1)).astype(F32).astype(BF16)
    got = split(gath[...].reshape(C * MOST, gath.shape[2]))
    high = dot(place, got[0])
    low = dot(place, got[1])
    p2 = (high.astype(BF16), low.astype(BF16))
    hl = dot(p2[0], p2[1], NT)
    part2[:, :panel] = dot(p2[0], p2[0], NT) + (hl + jnp.transpose(hl))
    part2[:, panel:] = dot3(p2, t2)
    second = scatter(part2, in2, psh, s2_send, s2_recv)

    phi_o[...] = jnp.transpose(high).astype(BF16)
    plo_o[...] = jnp.transpose(low).astype(BF16)

    for cp in first:
        cp.wait_recv()
    total = part1[pl.ds(pl.multiple_of(r * share, 8), share)]
    for d in range(1, R):
        total += in1[d - 1]
    sketch_o[...] = total[:, :cols_dev]
    gtrail_o[...] = total[:, cols_dev:]
    e3 = (prow[:1, :] - c * cols_dev == lax.broadcasted_iota(jnp.int32, (cols_dev, panel), 0)).astype(F32)
    gpbuf[0] = full_dot(total[:, :cols_dev], e3)
    third = []
    for d in range(1, C):
        cp = pltpu.make_async_remote_copy(
            gpbuf.at[0], gpbuf.at[d], p_send.at[d - 1], p_recv.at[d - 1],
            device_id=(r, lax.rem(c + d, C)), device_id_type=MESH)
        cp.start()
        third.append(cp)

    for cp in second:
        cp.wait_recv()
    mine = pl.ds(pl.multiple_of(r * psh, 8), psh)
    total2 = part2[mine]
    for d in range(1, R):
        total2 += in2[d - 1]
    full[mine] = total2
    fourth = []
    for d in range(1, R):
        cp = pltpu.make_async_remote_copy(
            full.at[mine], full.at[mine], a_send.at[d - 1], a_recv.at[d - 1],
            device_id=(lax.rem(r + d, R), c), device_id_type=MESH)
        cp.start()
        fourth.append(cp)

    for cp in third:
        cp.wait_recv()
    gp = gpbuf[0]
    for d in range(1, C):
        gp += gpbuf[d]
    gpan_o[...] = gp
    for cp in fourth:
        cp.wait_recv()
    sums_o[...] = full[...]
    for cp in list(across.values()) + waits + relays + first + second + third + fourth:
        cp.wait_send()


def ordered(place, values):
    high = values.astype(BF16)
    rest = values - high.astype(F32)
    mid = rest.astype(BF16)
    low = (rest - mid.astype(F32)).astype(BF16)
    return (dot(place, low) + dot(place, mid)) + dot(place, high)


def gather_by_halves(R, C, mat, gau_in, piv, trl_in, sketch_o, gtrail_o, gpan_o, sums_o, phi_o, plo_o, place_o,
                     gau, trl, hbuf, lbuf, inx, pairs, gath, part1, near, far, in1, in_near, in_far, full_near, full_far, diag, gpbuf,
                     l_sem, x_send, x_recv, g_send, g_recv, y_send, y_recv, f_send, f_recv, s_send, s_recv, n_send, n_recv,
                     o_send, o_recv, an_send, an_recv, ao_send, ao_recv, p_send, p_recv, d_send, d_recv):
    r, c = lax.axis_index("rows"), lax.axis_index("cols")
    cols_dev, panel = mat.shape[1], piv.shape[1]
    depth = mat.shape[0]
    share = gau.shape[0] // R
    half = panel // 2
    hsh = half // R
    y, k = c // 2, c % 2
    partner = c + 1 - 2 * k
    opposite = lax.rem(c + 2, C)

    loads = [pltpu.make_async_copy(trl_in, trl, l_sem.at[0]), pltpu.make_async_copy(gau_in, gau, l_sem.at[1])]
    for cp in loads:
        cp.start()
    barrier = pltpu.get_barrier_semaphore()
    for d in range(1, C):
        pl.semaphore_signal(barrier, inc=1, device_id=(r, lax.rem(c + d, C)), device_id_type=MESH)
    for d in range(1, R):
        pl.semaphore_signal(barrier, inc=1, device_id=(lax.rem(r + d, R), c), device_id_type=MESH)

    prow = jnp.broadcast_to(piv[...], (panel, panel))
    pcol = jnp.transpose(prow.astype(F32)).astype(jnp.int32)
    brow = jnp.zeros_like(prow)
    bcol = jnp.zeros_like(prow)
    for b in range(1, C):
        brow += (prow >= b * cols_dev).astype(jnp.int32)
        bcol += (pcol >= b * cols_dev).astype(jnp.int32)
    sub = lax.broadcasted_iota(jnp.int32, (panel, panel), 0)
    lane = lax.broadcasted_iota(jnp.int32, (panel, panel), 1)
    same = brow == bcol
    rank_row = jnp.sum(jnp.where(same & (sub < lane), 1.0, 0.0), axis=0, keepdims=True)
    rank_col = jnp.sum(jnp.where(same & (lane < sub), 1.0, 0.0), axis=1, keepdims=True)
    slot_row = brow[:1, :] * MOST + rank_row.astype(jnp.int32)
    slot_col = bcol[:, :1] * MOST + rank_col.astype(jnp.int32)
    e1 = (slot_row - c * MOST == lax.broadcasted_iota(jnp.int32, (MOST, panel), 0)).astype(F32).astype(BF16)
    e2 = (pcol[:, :1] - c * cols_dev == lax.broadcasted_iota(jnp.int32, (panel, cols_dev), 1)).astype(F32).astype(BF16)
    sel = dot(e1, e2).astype(BF16)
    m2 = split(mat[...])
    gath[c] = dot(sel, m2[0], NT) + dot(sel, m2[1], NT)

    pl.semaphore_wait(barrier, C - 1 + R - 1)

    def block_copy(source, q, target, send, recv):
        piece = gath.at[source, pl.ds(q * (MOST // PARTS), MOST // PARTS)]
        return pltpu.make_async_remote_copy(piece, piece, send, recv, device_id=(r, target), device_id_type=MESH)

    def scatter(part, into, rows, send, recv):
        out = []
        for d in range(1, R):
            p = lax.rem(r + d, R)
            cp = pltpu.make_async_remote_copy(
                part.at[pl.ds(pl.multiple_of(p * rows, 8), rows)], into.at[d - 1], send.at[d - 1], recv.at[d - 1],
                device_id=(p, c), device_id_type=MESH)
            cp.start()
            out.append(cp)
        return out

    def finish(copies, part, into, rows):
        for cp in copies:
            cp.wait_recv()
        total = part[pl.ds(pl.multiple_of(r * rows, 8), rows)]
        for d in range(1, R):
            total += into[d - 1]
        return total

    def spread(total, whole, rows, send, recv):
        mine = pl.ds(pl.multiple_of(r * rows, 8), rows)
        whole[mine] = total
        out = []
        for d in range(1, R):
            cp = pltpu.make_async_remote_copy(
                whole.at[mine], whole.at[mine], send.at[d - 1], recv.at[d - 1],
                device_id=(lax.rem(r + d, R), c), device_id_type=MESH)
            cp.start()
            out.append(cp)
        return out

    across = [block_copy(c, q, opposite, y_send.at[q], y_recv.at[q]) for q in range(PARTS)]
    beside = [block_copy(c, q, partner, g_send.at[q], g_recv.at[q]) for q in range(PARTS)]
    relays = [block_copy(opposite, q, partner, f_send.at[q], f_recv.at[q]) for q in range(PARTS)]
    for cp in across + beside:
        cp.start()

    loads[0].wait()
    t2 = split(trl[...])
    for cp in beside:
        cp.wait_recv()
    own = gath[pl.ds(2 * y, 2)].reshape(half, depth)
    o2 = split(own)
    near[:, :half] = dot3(o2, o2, NT)
    near[:, half:] = dot3(o2, t2)
    near_out = scatter(near, in_near, hsh, n_send, n_recv)

    loads[1].wait()
    g2 = split(gau[...])
    part1[:, :cols_dev] = dot3(g2, m2)
    part1[:, cols_dev:] = dot3(g2, t2)
    side = lax.rem(r, 2)
    pair_out = []
    for i in range(R // 2):
        cp = pltpu.make_async_remote_copy(
            part1.at[pl.ds(pl.multiple_of((2 * i + 1 - side) * share, 8), share)], inx.at[i], x_send.at[i], x_recv.at[i],
            device_id=(r + 1 - 2 * side, c), device_id_type=MESH)
        cp.start()
        pair_out.append(cp)

    near_all = spread(finish(near_out, near, in_near, hsh), full_near, hsh, an_send, an_recv)
    across[0].wait_recv()
    relays[0].start()
    for cp in pair_out:
        cp.wait_recv()
    for i in range(R // 2):
        pairs[i] = part1[pl.ds(pl.multiple_of((2 * i + side) * share, 8), share)] + inx[i]
    sketch_out = []
    for d in range(1, R // 2):
        to = lax.rem(r // 2 + d, R // 2)
        cp = pltpu.make_async_remote_copy(
            pairs.at[to], in1.at[d - 1], s_send.at[d - 1], s_recv.at[d - 1],
            device_id=(2 * to + side, c), device_id_type=MESH)
        cp.start()
        sketch_out.append(cp)
    for q in range(1, PARTS):
        if q == PARTS - 1:
            own_t = jnp.transpose(own)
            t_high, t_low = split(own_t)
            hbuf[:, :half] = t_high
            lbuf[:, :half] = t_low
        across[q].wait_recv()
        relays[q].start()
    for cp in near_all:
        cp.wait_recv()
    swap = pltpu.make_async_remote_copy(
        full_near.at[:, pl.ds(0, half)], diag, d_send.at[0], d_recv.at[0],
        device_id=(r, opposite), device_id_type=MESH)
    swap.start()
    for cp in relays:
        cp.wait_recv()

    other = gath[pl.ds(2 * (1 - y), 2)].reshape(half, depth)
    r2 = split(other)
    far[:, :half] = dot3(r2, o2, NT)
    far[:, half:] = dot3(r2, t2)
    far_out = scatter(far, in_far, hsh, o_send, o_recv)

    r_high, r_low = split(jnp.transpose(other))
    hbuf[:, half:] = r_high
    lbuf[:, half:] = r_low
    stores = [pltpu.make_async_copy(hbuf, phi_o, l_sem.at[2]), pltpu.make_async_copy(lbuf, plo_o, l_sem.at[3])]
    for cp in stores:
        cp.start()
    slot = lane + half * y
    slot = jnp.where(slot >= panel, slot - panel, slot)
    place = (slot_col == slot).astype(F32).astype(BF16)
    place_o[...] = place

    far_all = spread(finish(far_out, far, in_far, hsh), full_far, hsh, ao_send, ao_recv)

    for cp in sketch_out:
        cp.wait_recv()
    total = pairs[r // 2]
    for d in range(1, R // 2):
        total += in1[d - 1]
    sketch_o[...] = total[:, :cols_dev]
    gtrail_o[...] = total[:, cols_dev:]
    e3 = (prow[:1, :] - c * cols_dev == lax.broadcasted_iota(jnp.int32, (cols_dev, panel), 0)).astype(F32)
    gpbuf[0] = full_dot(total[:, :cols_dev], e3)
    third = []
    for d in range(1, C):
        cp = pltpu.make_async_remote_copy(
            gpbuf.at[0], gpbuf.at[d], p_send.at[d - 1], p_recv.at[d - 1],
            device_id=(r, lax.rem(c + d, C)), device_id_type=MESH)
        cp.start()
        third.append(cp)
    swap.wait_recv()
    for cp in far_all:
        cp.wait_recv()
    mixed = full_far[:, :half]
    first_rows = jnp.concatenate([full_near[:, :half], jnp.transpose(mixed), full_near[:, half:]], axis=1)
    last_rows = jnp.concatenate([mixed, diag[...], full_far[:, half:]], axis=1)
    by_rows = ordered(place, jnp.concatenate([first_rows, last_rows], axis=0))
    sums_o[:, panel:] = by_rows[:, panel:]
    sums_o[:, :panel] = ordered(place, jnp.transpose(by_rows[:, :panel]))
    for cp in third:
        cp.wait_recv()
    gp = gpbuf[0]
    for d in range(1, C):
        gp += gpbuf[d]
    gpan_o[...] = gp
    for cp in across + beside + relays + near_out + pair_out + sketch_out + near_all + far_out + far_all + third + [swap]:
        cp.wait_send()
    for cp in stores:
        cp.wait()


def factor_inverse(a):
    n = a.shape[0]
    rows = lax.broadcasted_iota(jnp.int32, (8, n), 0)
    lanes = lax.broadcasted_iota(jnp.int32, (8, n), 1)
    left = [a[8 * b:8 * b + 8, :] for b in range(n // 8)]
    right = [jnp.where(lanes == rows + 8 * b, 1.0, 0.0) for b in range(n // 8)]
    out = []
    for b0 in range(n // 8):
        x, y = left[b0], right[b0]
        cols = [jnp.broadcast_to(x[:, 8 * b0 + i:8 * b0 + i + 1], (8, n)) for i in range(8)]
        done = []
        for s in range(0, 8, 2):
            c0, c1 = cols[s], cols[s + 1]
            p, q, t = c0[s:s + 1], c0[s + 1:s + 2], c1[s + 1:s + 2]
            det = p * t - q * q
            inv = 1.0 / det
            ip, iq, it = t * inv, -q * inv, p * inv
            y0, y1 = y[s:s + 1], y[s + 1:s + 2]
            done.append(y0 * lax.rsqrt(p))
            done.append((y1 - (q / p) * y0) * lax.rsqrt(det / p))

            def eliminate(block):
                r0, r1 = block[s:s + 1], block[s + 1:s + 2]
                u0, u1 = ip * r0 + iq * r1, iq * r0 + it * r1
                return jnp.where(rows == s, u0, jnp.where(rows == s + 1, u1, block - c0 * u0 - c1 * u1))

            for i in range(s + 2, 8):
                cols[i] = eliminate(cols[i])
            x, y = eliminate(x), eliminate(y)
        out.append(jnp.concatenate(done, axis=0))
        for b in range(b0 + 1, n // 8):
            across = [jnp.broadcast_to(left[b][:, 8 * b0 + i:8 * b0 + i + 1], (8, n)) for i in range(8)]
            for i in range(8):
                left[b] = left[b] - across[i] * x[i:i + 1]
                right[b] = right[b] - across[i] * y[i:i + 1]
    return jnp.concatenate(out, axis=0)


def solve_and_project(sums, gtrail, gpan, place, sketch, phi, plo, trl, sketch_o, coupling_o, projected_o, tsk_o, hbuf, lbuf, tbuf, sems):
    copies = [pltpu.make_async_copy(a, b, sems.at[i])
              for i, (a, b) in enumerate(((phi, hbuf), (plo, lbuf), (trl, tbuf)))]
    for cp in copies:
        cp.start()
    sketch_o[...] = sketch[...]
    n = sums.shape[0]
    h = n // 2
    c1, c2 = sums[:h, n:], sums[h:, n:]
    i1 = factor_inverse(sums[:h, :h])
    l21 = full_dot(sums[h:, :h], i1, NT)
    k1 = full_dot(i1, c1)
    i2 = factor_inverse(sums[h:, h:n] - full_dot(l21, l21, NT))
    k2 = full_dot(i2, c2 - full_dot(l21, k1))
    coupling_o[:h, :] = k1
    coupling_o[h:, :] = k2
    w2 = full_dot(jnp.transpose(i2), k2)
    w1 = full_dot(jnp.transpose(i1), k1 - full_dot(jnp.transpose(l21), w2))
    weights = jnp.concatenate([w1, w2], axis=0)
    tsk_o[...] = gtrail[...] - full_dot(gpan[...], weights)
    w = tuple(dot(place[...], piece, TN).astype(BF16) for piece in split(weights))
    for cp in copies:
        cp.wait()
    projected_o[...] = tbuf[...] - dot3((hbuf[...], lbuf[...]), w)


def shards(R, C, matrix, gaussian, pivots, trailing):
    depth, cols_dev = matrix.shape
    sketch_rows = gaussian.shape[0]
    panel = pivots.shape[0]
    slab = trailing.shape[1]
    share, psh = sketch_rows // R, panel // R
    ny = max(C // 2 - 1, 1)
    vm = pl.BlockSpec(memory_space=pltpu.VMEM)
    anywhere = pl.BlockSpec(memory_space=pl.ANY)
    dma = pltpu.SemaphoreType.DMA
    if C == 4 and R % 2 == 0 and C * MOST == panel and panel == 2 * slab and (panel // 2) % (8 * R) == 0:
        half = panel // 2
        sketch, gtrail, gpan, sums, phi, plo, place = pl.pallas_call(
            functools.partial(gather_by_halves, R, C),
            out_shape=[
                jax.ShapeDtypeStruct((share, cols_dev), F32),
                jax.ShapeDtypeStruct((share, slab), F32),
                jax.ShapeDtypeStruct((share, panel), F32),
                jax.ShapeDtypeStruct((panel, panel + slab), F32),
                jax.ShapeDtypeStruct((depth, panel), BF16),
                jax.ShapeDtypeStruct((depth, panel), BF16),
                jax.ShapeDtypeStruct((panel, panel), BF16),
            ],
            in_specs=[vm, anywhere, vm, anywhere],
            out_specs=[vm] * 4 + [anywhere] * 2 + [vm],
            scratch_shapes=[
                pltpu.VMEM((sketch_rows, depth), F32),
                pltpu.VMEM((depth, slab), F32),
                pltpu.VMEM((depth, panel), BF16),
                pltpu.VMEM((depth, panel), BF16),
                pltpu.VMEM((R // 2, share, cols_dev + slab), F32),
                pltpu.VMEM((R // 2, share, cols_dev + slab), F32),
                pltpu.VMEM((C, MOST, depth), F32),
                pltpu.VMEM((sketch_rows, cols_dev + slab), F32),
                pltpu.VMEM((half, half + slab), F32),
                pltpu.VMEM((half, half + slab), F32),
                pltpu.VMEM((R - 1, share, cols_dev + slab), F32),
                pltpu.VMEM((R - 1, half // R, half + slab), F32),
                pltpu.VMEM((R - 1, half // R, half + slab), F32),
                pltpu.VMEM((half, half + slab), F32),
                pltpu.VMEM((half, half + slab), F32),
                pltpu.VMEM((half, half), F32),
                pltpu.VMEM((C, share, panel), F32),
                dma((4,)),
                *[dma((R // 2,))] * 2,
                *[dma((PARTS,))] * 6,
                *[dma((R - 1,))] * 10,
                *[dma((C - 1,))] * 2,
                *[dma((1,))] * 2,
            ],
            compiler_params=pltpu.CompilerParams(
                collective_id=0, has_side_effects=True, vmem_limit_bytes=56 * 1024 * 1024),
        )(matrix, gaussian, pivots.reshape(1, panel), trailing)
    else:
        sketch, gtrail, gpan, sums, phi, plo = pl.pallas_call(
            functools.partial(gather_and_sum, R, C),
            out_shape=[
                jax.ShapeDtypeStruct((share, cols_dev), F32),
                jax.ShapeDtypeStruct((share, slab), F32),
                jax.ShapeDtypeStruct((share, panel), F32),
                jax.ShapeDtypeStruct((panel, panel + slab), F32),
                jax.ShapeDtypeStruct((depth, panel), BF16),
                jax.ShapeDtypeStruct((depth, panel), BF16),
            ],
            in_specs=[vm] * 4,
            out_specs=[vm] * 6,
            scratch_shapes=[
                pltpu.VMEM((C, MOST, depth), F32),
                pltpu.VMEM((sketch_rows, cols_dev + slab), F32),
                pltpu.VMEM((panel, panel + slab), F32),
                pltpu.VMEM((R - 1, share, cols_dev + slab), F32),
                pltpu.VMEM((R - 1, psh, panel + slab), F32),
                pltpu.VMEM((panel, panel + slab), F32),
                pltpu.VMEM((C, share, panel), F32),
                dma((PARTS,)), dma((PARTS,)),
                dma((ny, PARTS)), dma((ny, PARTS)),
                dma((ny, PARTS)), dma((ny, PARTS)),
                dma((R - 1,)), dma((R - 1,)),
                dma((R - 1,)), dma((R - 1,)),
                dma((R - 1,)), dma((R - 1,)),
                dma((C - 1,)), dma((C - 1,)),
            ],
            compiler_params=pltpu.CompilerParams(
                collective_id=0, has_side_effects=True, vmem_limit_bytes=56 * 1024 * 1024),
        )(matrix, gaussian, pivots.reshape(1, panel), trailing)
        place = jnp.eye(panel, dtype=BF16)
    return pl.pallas_call(
        solve_and_project,
        out_shape=[
            jax.ShapeDtypeStruct((share, cols_dev), F32),
            jax.ShapeDtypeStruct((panel, slab), F32),
            jax.ShapeDtypeStruct((depth, slab), F32),
            jax.ShapeDtypeStruct((share, slab), F32),
        ],
        in_specs=[vm] * 5 + [anywhere] * 3,
        out_specs=[vm] * 4,
        scratch_shapes=[
            pltpu.VMEM((depth, panel), BF16),
            pltpu.VMEM((depth, panel), BF16),
            pltpu.VMEM((depth, slab), F32),
            dma((3,)),
        ],
        compiler_params=pltpu.CompilerParams(vmem_limit_bytes=56 * 1024 * 1024),
    )(sums, gtrail, gpan, place, sketch, phi, plo, trailing)


def solution(mesh):
    placed = (P("rows", "cols"), P(None, "rows"), P(), P("rows", "cols"))
    return jax.shard_map(
        functools.partial(shards, mesh.shape["rows"], mesh.shape["cols"]),
        mesh=mesh,
        in_specs=placed,
        out_specs=(P("rows", "cols"), P(None, "cols"), P("rows", "cols"), P("rows", "cols")),
        check_vma=False,
    )
```
